128 devices in a mesh: op: 8 (over z, core), sec: 16 (over y, x).
Axes of the slice: x: 4, y: 4, z: 4, core: 2. Of those that a mesh axis runs over, the one named last changes fastest.
Arguments:
- psi: bfloat16 [256, 256, 256], P('sec'), may hold values from -2 to 2
- left_ops: bfloat16 [64, 256, 256], P('op', 'sec'), may hold values from -0.375 to 0.375
- right_ops: bfloat16 [64, 256, 256], P('op'), may hold values from -0.375 to 0.375
- op_shift: int32 [64], P('op'), may hold values from -2 to 2, as said below
- sector_dims: int32 [256], P('sec'), may hold values from 64 to 256, as said below
Outputs:
- sigma: bfloat16 [256, 256, 256], P('sec', 'op')
The draws below stay inside these ranges and needn't reach their ends.
Inputs may be any that keep to these rules, and one draw needn't show every extreme that they name: `op_shift`: every value from -2 to 2 occurs. `sector_dims`: some sector has 256 live rows and some has 64.
All inputs are finite; a program needn't handle non-finite values.
Results may differ from the reference program's by a relative error of at most 0.0049.
Values may be sent and summed in bfloat16 or wider, within the bound.
No kernel may reach another device: no remote copies, remote signals or barrier semaphores. Data moves between devices by JAX's collectives and lax.ppermute only.
A program may use at most 64 MiB of HBM per device.

```python
import jax
import jax.numpy as jnp
from jax import lax

B = 256
K = 64
QMAX = 2
S = 256


def draw_op_shift(key, part):
    key = jax.random.fold_in(key, 11)
    order = jax.random.permutation(key, K)
    return (order % (2 * QMAX + 1) - QMAX).astype(jnp.int32)


def draw_sector_dims(key, part):
    key = jax.random.fold_in(key, 23)
    first_key, second_key = jax.random.split(key)
    dims_drawn = jax.random.randint(first_key, (S,), B // 4, B + 1)
    order = jax.random.permutation(second_key, S)
    dims_drawn = dims_drawn.at[order[0]].set(B)
    dims_drawn = dims_drawn.at[order[1]].set(B // 4)
    return dims_drawn.astype(jnp.int32)


def level_of(rng, dims, shards, smallest, top_value):
    factor_of = 1.0
    for axis_at, parts in shards:
        steps = jax.random.uniform(jax.random.fold_in(jax.random.fold_in(rng, 6), axis_at), (parts,), jnp.float32, smallest / len(shards), top_value / len(shards))
        factor_of = factor_of * jnp.repeat(jnp.exp(steps), dims[axis_at] // parts).reshape((-1,) + (1,) * (len(dims) - 1 - axis_at))
    return factor_of


def centred(key, dims, deviation, bound, cuts=(), kind=jnp.bfloat16):
    entries = jax.random.normal(key, dims, jnp.float32) * deviation
    if len(cuts) > 0:
        entries = level_of(key, dims, cuts, -0.22, 0.18) * entries
    return jnp.clip(entries, min=-bound, max=bound).astype(kind)


def setup_inputs(seed: int = 0) -> dict:
    streams_of = jax.random.split(jax.random.key(seed), 6)
    psi = centred(streams_of[0], (S, B, B), 0.25, 2.0, ((0, 16),))
    left_ops = centred(streams_of[1], (K, B, B), B ** -0.5, 0.375, ((0, 8), (1, 16)))
    right_ops = centred(streams_of[2], (K, B, B), B ** -0.5, 0.375, ((0, 8),))
    op_shift = draw_op_shift(jax.random.fold_in(streams_of[5], 71), 0)
    sector_dims = draw_sector_dims(jax.random.fold_in(streams_of[5], 71), 0)
    return {"psi": psi, "left_ops": left_ops, "right_ops": right_ops, "op_shift": op_shift, "sector_dims": sector_dims}


def reference(psi, left_ops, right_ops, op_shift, sector_dims):
    row_index = jnp.arange(B, dtype=jnp.int32)
    live_mask = (row_index[None, :] < sector_dims[:, None]).astype(jnp.bfloat16)
    masked = psi * live_mask[:, :, None] * live_mask[:, None, :]
    masked_wide = masked.astype(jnp.float32)

    def one_operator(accumulated, source_item):
        left_factor, right_factor, charge = source_item
        product = jnp.einsum("ai,sij->saj", left_factor.astype(jnp.float32), masked_wide).astype(jnp.bfloat16)
        images = jnp.einsum("saj,bj->sab", product.astype(jnp.float32), right_factor.astype(jnp.float32))
        padded = jnp.pad(images, ((QMAX, QMAX), (0, 0), (0, 0)))
        moved = jnp.roll(padded, charge, axis=0)[QMAX:QMAX + S]
        return accumulated + moved, None

    start_value = jnp.zeros((S, B, B), jnp.float32)
    summed, _ = lax.scan(one_operator, start_value, (left_ops, right_ops, op_shift))
    live_wide = live_mask.astype(jnp.float32)
    return (summed * live_wide[:, :, None] * live_wide[:, None, :]).astype(jnp.bfloat16)
```

```python
import functools

import jax
import jax.numpy as jnp
from jax import lax
from jax.experimental import pallas as pl
from jax.experimental.pallas import tpu as pltpu
from jax.sharding import PartitionSpec as P

NZ, NC, NY, NX = 4, 2, 4, 4
B = 256
OPS = 8
SECS = 16
QMAX = 2
BF = jnp.bfloat16
F32 = jnp.float32
NT = (((1,), (1,)), ((), ()))


def flat(z, c, y, x):
    return ((z * NC + c) * NY + y) * NX + x


def move(block, target):
    route = []
    for z in range(NZ):
        for c in range(NC):
            for y in range(NY):
                for x in range(NX):
                    to = target(z, c, y, x)
                    if to is not None:
                        route.append((flat(z, c, y, x), flat(*to)))
    return lax.ppermute(block, ("op", "sec"), route)


def gather_first(d):
    return lambda z, c, y, x: (z, c, y, (x + d) % NX) if c == 0 else (z, c, (y + d) % NY, x)


def gather_second(d):
    return lambda z, c, y, x: (z, c, (y + d) % NY, x) if c == 0 else (z, c, y, (x + d) % NX)


def edge_target(z, c, y, x):
    q = y * NX + x + (1 if c == 0 else -1)
    return (z, c, q // NX, q % NX) if 0 <= q < NX * NY else None


def other_core(z, c, y, x):
    return (z, 1 - c, y, x)


def along_z(sign):
    return lambda z, c, y, x: ((z + (sign if c == 0 else -sign)) % NZ, c, y, x)


def first_product(shift_ref, dims_ref, psi_ref, right_ref, h_ref, masked_ref):
    rows = lax.broadcasted_iota(jnp.int32, (B, B), 0)
    cols = lax.broadcasted_iota(jnp.int32, (B, B), 1)

    def mask_one(s, _):
        d = dims_ref[s]
        keep = (rows < d) & (cols < d)
        masked_ref[s] = jnp.where(keep, psi_ref[s].astype(F32), 0.0).astype(BF)
        return 0

    lax.fori_loop(0, SECS, mask_one, 0)

    def one_target(t, _):
        for o in range(OPS):
            s = t - shift_ref[o]
            inside = (s >= 0) & (s < SECS)

            @pl.when(inside)
            def _():
                h = lax.dot_general(masked_ref[s], right_ref[o], NT, preferred_element_type=F32)
                h_ref[t, o * B:(o + 1) * B, :] = h.astype(BF)

            @pl.when(jnp.logical_not(inside))
            def _():
                h_ref[t, o * B:(o + 1) * B, :] = jnp.zeros((B, B), BF)
        return 0

    lax.fori_loop(0, SECS, one_target, 0)


def second_product(shift_ref, place_ref, t0, t1, t2, t3, edge_ref, right_ref, h_ref,
                   mine_ref, other_ref, left_ref, total_ref):
    t = pl.program_id(0)
    z, core, y, x = place_ref[0], place_ref[1], place_ref[2], place_ref[3]

    @pl.when(t == 0)
    def _():
        for e, block in enumerate((t0, t1, t2, t3)):
            for d in range(4):
                back_y = jnp.where(core == 0, e, d)
                back_x = jnp.where(core == 0, d, e)
                q = ((y - back_y + NY) % NY) * NX + (x - back_x + NX) % NX
                start = pl.multiple_of(q * 16, 16)
                for o in range(OPS):
                    left_ref[pl.ds(start, 16), o * B:(o + 1) * B] = block[d, o]

    total_ref[...] = jnp.dot(left_ref[...], h_ref[0], preferred_element_type=F32)

    @pl.when((t < QMAX) | (t >= SECS - QMAX))
    def _():
        for o in range(OPS):
            s = t - shift_ref[o]

            @pl.when((s < 0) | (s >= SECS))
            def _():
                e = jnp.where(s < 0, s + QMAX, s - SECS + QMAX)
                h = lax.dot_general(edge_ref[e], right_ref[o], NT, preferred_element_type=F32)
                total_ref[...] += jnp.dot(left_ref[:, o * B:(o + 1) * B], h.astype(BF), preferred_element_type=F32)

    for p in range(NZ * NC):
        to_z, to_core = p // 2, p % 2
        ahead = (to_z - z + NZ) % NZ if to_core == 0 else (z - to_z + NZ) % NZ

        @pl.when(core == to_core)
        def _():
            mine_ref[ahead, 0] = total_ref[p * 32:(p + 1) * 32, :]

        @pl.when(core != to_core)
        def _():
            other_ref[ahead, 0] = total_ref[p * 32:(p + 1) * 32, :].astype(BF)


def on_device(psi, left_ops, right_ops, op_shift, sector_dims):
    p, q = lax.axis_index("op"), lax.axis_index("sec")
    core = p % NC
    place = jnp.stack([p // NC, core, q // NX, q % NX]).astype(jnp.int32)
    index = jnp.arange(B, dtype=jnp.int32)

    ends = jnp.where(core == 0, psi[SECS - QMAX:], psi[:QMAX])
    end_dims = jnp.where(core == 0, sector_dims[SECS - QMAX:], sector_dims[:QMAX])
    live = (index[None, :] < end_dims[:, None])
    ends = jnp.where(live[:, :, None] & live[:, None, :], ends, jnp.zeros((), BF))

    firsts = [left_ops] + [move(left_ops, gather_first(d)) for d in (1, 3, 2)]
    edge_in = move(ends, edge_target)
    strips = jnp.stack([firsts[0], firsts[1], firsts[3], firsts[2]])
    seconds = [move(strips, gather_second(d)) for d in (1, 3, 2)]
    t0, t1, t3, t2 = strips, *seconds
    edge_other = move(edge_in, other_core)
    edges = jnp.where(core == 0, jnp.concatenate([edge_in, edge_other]), jnp.concatenate([edge_other, edge_in]))

    smem = pl.BlockSpec(memory_space=pltpu.SMEM)
    vmem = pl.BlockSpec(memory_space=pltpu.VMEM)
    flops = 2 * OPS * SECS * B * B * B
    h = pl.pallas_call(
        first_product,
        out_shape=jax.ShapeDtypeStruct((SECS, OPS * B, B), BF),
        in_specs=[smem, smem, vmem, vmem],
        out_specs=vmem,
        scratch_shapes=[pltpu.VMEM((SECS, B, B), BF)],
        compiler_params=pltpu.CompilerParams(vmem_limit_bytes=40 << 20),
        cost_estimate=pl.CostEstimate(flops=flops, bytes_accessed=20 << 20, transcendentals=0),
        name="first_product",
    )(op_shift, sector_dims, psi, right_ops)

    def whole(*shape):
        return pl.BlockSpec(shape, lambda t: (0,) * len(shape))

    strip = whole(4, OPS, 16, B)
    mine, other = pl.pallas_call(
        second_product,
        grid=(SECS,),
        out_shape=[jax.ShapeDtypeStruct((NZ, SECS, 32, B), F32), jax.ShapeDtypeStruct((NZ, SECS, 32, B), BF)],
        in_specs=[smem, smem, strip, strip, strip, strip, whole(2 * QMAX, B, B), whole(OPS, B, B),
                  pl.BlockSpec((1, OPS * B, B), lambda t: (t, 0, 0))],
        out_specs=[pl.BlockSpec((NZ, 1, 32, B), lambda t: (0, t, 0, 0))] * 2,
        scratch_shapes=[pltpu.VMEM((B, OPS * B), BF), pltpu.VMEM((B, B), F32)],
        compiler_params=pltpu.CompilerParams(vmem_limit_bytes=40 << 20),
        cost_estimate=pl.CostEstimate(flops=flops, bytes_accessed=24 << 20, transcendentals=0),
        name="second_product",
    )(op_shift, place, t0, t1, t2, t3, edges, right_ops, h)

    total = mine + move(other, other_core).astype(F32)
    far = move(total[2].astype(BF), along_z(1))
    back = move(total[3].astype(BF), along_z(-1))
    near = move((total[1] + far.astype(F32)).astype(BF), along_z(1))
    summed = total[0] + back.astype(F32) + near.astype(F32)
    live = index[None, :] < sector_dims[:, None]
    mine_rows = p * 32 + jnp.arange(32, dtype=jnp.int32)
    live_rows = mine_rows[None, :] < sector_dims[:, None]
    return jnp.where(live_rows[:, :, None] & live[:, None, :], summed, 0.0).astype(BF)


def solution(mesh):
    placed = (P("sec", None, None), P("op", "sec", None), P("op", None, None), P("op"), P("sec"))
    return jax.shard_map(
        on_device, mesh=mesh, in_specs=placed, out_specs=P("sec", "op", None), check_vma=False
    )
```

```python
import jax
import jax.numpy as jnp
from jax import lax
from jax.experimental import pallas as pl
from jax.experimental.pallas import tpu as pltpu
from jax.sharding import PartitionSpec as P

NZ, NC, NY, NX = 4, 2, 4, 4
B = 256
OPS = 8
SECS = 16
QMAX = 2
HELD = SECS + 2 * QMAX
BF = jnp.bfloat16
F32 = jnp.float32


def flat(z, c, y, x):
    return ((z * NC + c) * NY + y) * NX + x


def move(block, target):
    route = []
    for z in range(NZ):
        for c in range(NC):
            for y in range(NY):
                for x in range(NX):
                    to = target(z, c, y, x)
                    if to is not None:
                        route.append((flat(z, c, y, x), flat(*to)))
    return lax.ppermute(block, ("op", "sec"), route)


def gather_first(d):
    return lambda z, c, y, x: (z, c, y, (x + d) % NX) if c == 0 else (z, c, (y + d) % NY, x)


def gather_second(d):
    return lambda z, c, y, x: (z, c, (y + d) % NY, x) if c == 0 else (z, c, y, (x + d) % NX)


def edge_target(z, c, y, x):
    q = y * NX + x + (1 if c == 0 else -1)
    return (z, c, q // NX, q % NX) if 0 <= q < NX * NY else None


def other_core(z, c, y, x):
    return (z, 1 - c, y, x)


def along_z(sign):
    return lambda z, c, y, x: ((z + (sign if c == 0 else -sign)) % NZ, c, y, x)


def mask_sectors(dims_ref, place_ref, psi_ref, masked_ref, ends_ref):
    rows = lax.broadcasted_iota(jnp.int32, (B, B), 0)
    cols = lax.broadcasted_iota(jnp.int32, (B, B), 1)

    def mask_one(s, _):
        d = dims_ref[s]
        keep = (rows < d) & (cols < d)
        masked_ref[s] = jnp.where(keep, psi_ref[s].astype(F32), 0.0).astype(BF)
        return 0

    lax.fori_loop(0, SECS, mask_one, 0)
    start = (1 - place_ref[1]) * (SECS - QMAX)
    for e in range(QMAX):
        ends_ref[e] = masked_ref[start + e]


def stack_strips(s0, s1, s2, s3, out_ref):
    for d, strip in enumerate((s0, s1, s2, s3)):
        out_ref[d] = strip[...]


def own_sectors(masked_ref, right_ref, h_ref):
    def one_operator(o, _):
        right_t = right_ref[o].T
        for s in range(0, SECS, 4):
            h = jnp.dot(masked_ref[s:s + 4].reshape(4 * B, B), right_t, preferred_element_type=F32)
            h_ref[o, (s + QMAX) * B:(s + QMAX + 4) * B, :] = h.astype(BF)
        return 0

    lax.fori_loop(0, OPS, one_operator, 0)


def edge_sectors(place_ref, edge_in, edge_other, right_ref, _, h_ref):
    below = place_ref[1] * (SECS + QMAX) * B

    def one_operator(o, _):
        right_t = right_ref[o].T
        for edge, start in ((edge_in, below), (edge_other, (SECS + QMAX) * B - below)):
            h = jnp.dot(edge[...].reshape(QMAX * B, B), right_t, preferred_element_type=F32)
            h_ref[o, pl.ds(pl.multiple_of(start, B), QMAX * B), :] = h.astype(BF)
        return 0

    lax.fori_loop(0, OPS, one_operator, 0)


def second_product(shift_ref, place_ref, t0, t1, t2, t3, h_ref, mine_ref, other_ref, left_ref):
    z, core, y, x = place_ref[0], place_ref[1], place_ref[2], place_ref[3]
    for e, block in enumerate((t0, t1, t2, t3)):
        for d in range(4):
            row_y = (y - jnp.where(core == 0, e, d) + NY) % NY
            row_x = (x - jnp.where(core == 0, d, e) + NX) % NX
            q = row_y * NX + row_x
            to_z, to_core = q // 4, (q // 2) % 2
            ahead = jnp.where(to_core == 0, to_z - z + NZ, z - to_z + NZ) % NZ
            start = jnp.where(to_core == core, 0, B // 2) + ahead * 32 + (q % 2) * 16
            start = pl.multiple_of(start, 16)
            for o in range(OPS):
                left_ref[pl.ds(start, 16), o * B:(o + 1) * B] = block[d, o]

    def four_targets(i, _):
        for u in range(4):
            t = i * 4 + u
            sources = [
                h_ref[o, pl.ds(pl.multiple_of((t + QMAX - shift_ref[o]) * B, B), B), :] for o in range(OPS)
            ]
            total = jnp.dot(left_ref[...], jnp.concatenate(sources, axis=0), preferred_element_type=F32)
            for k in range(NZ):
                mine_ref[k, t] = total[k * 32:(k + 1) * 32]
                other_ref[k, t] = total[B // 2 + k * 32:B // 2 + (k + 1) * 32].astype(BF)
        return 0

    lax.fori_loop(0, SECS // 4, four_targets, 0)


def on_device(psi, left_ops, right_ops, op_shift, sector_dims):
    p, q = lax.axis_index("op"), lax.axis_index("sec")
    core = p % NC
    place = jnp.stack([p // NC, core, q // NX, q % NX]).astype(jnp.int32)
    index = jnp.arange(B, dtype=jnp.int32)

    smem = pl.BlockSpec(memory_space=pltpu.SMEM)
    vmem = pl.BlockSpec(memory_space=pltpu.VMEM)

    def call(kernel, name, in_specs, out_shape, dots, scratch=(), aliases={}):
        return pl.pallas_call(
            kernel, in_specs=in_specs, out_shape=[jax.ShapeDtypeStruct(*o) for o in out_shape],
            out_specs=[vmem] * len(out_shape), name=name, scratch_shapes=scratch, input_output_aliases=aliases,
            compiler_params=pltpu.CompilerParams(vmem_limit_bytes=4 << 20),
            cost_estimate=pl.CostEstimate(flops=2 * dots * B ** 3, bytes_accessed=4 << 20, transcendentals=0))

    place, left_ops = lax.optimization_barrier((place, left_ops))
    firsts = [left_ops] + [move(left_ops, gather_first(d)) for d in (1, 3, 2)]
    masked, ends = call(
        mask_sectors, "mask_sectors", [smem, smem, vmem],
        [((SECS, B, B), BF), ((QMAX, B, B), BF)], 0,
    )(sector_dims, place, psi)
    ends, *_ = lax.optimization_barrier((ends, *firsts[1:]))
    edge_in = move(ends, edge_target)
    strips, = call(stack_strips, "stack_strips", [vmem] * 4, [((4, OPS, 16, B), BF)], 0)(
        firsts[0], firsts[1], firsts[3], firsts[2])
    seconds = [move(strips, gather_second(d)) for d in (1, 3, 2)]
    t0, t1, t3, t2 = strips, *seconds
    edge_in, _ = lax.optimization_barrier((edge_in, strips))
    edge_other = move(edge_in, other_core)

    masked, _ = lax.optimization_barrier((masked, edge_in))
    h, = call(
        own_sectors, "own_sectors", [vmem] * 2, [((OPS, HELD * B, B), BF)], OPS * SECS,
    )(masked, right_ops)
    h, = call(
        edge_sectors, "edge_sectors", [smem] + [vmem] * 4, [((OPS, HELD * B, B), BF)], 1, aliases={4: 0},
    )(place, edge_in, edge_other, right_ops, h)
    mine, other = call(
        second_product, "second_product", [smem, smem] + [vmem] * 5,
        [((NZ, SECS, 32, B), F32), ((NZ, SECS, 32, B), BF)], OPS * SECS, [pltpu.VMEM((B, OPS * B), BF)],
    )(op_shift, place, t0, t1, t2, t3, h)

    total = mine + move(other, other_core).astype(F32)
    far = move(total[2].astype(BF), along_z(1))
    back = move(total[3].astype(BF), along_z(-1))
    near = move((total[1] + far.astype(F32)).astype(BF), along_z(1))
    summed = total[0] + back.astype(F32) + near.astype(F32)
    live = index[None, :] < sector_dims[:, None]
    mine_rows = p * 32 + jnp.arange(32, dtype=jnp.int32)
    live_rows = mine_rows[None, :] < sector_dims[:, None]
    return jnp.where(live_rows[:, :, None] & live[:, None, :], summed, 0.0).astype(BF)


def solution(mesh):
    placed = (P("sec", None, None), P("op", "sec", None), P("op", None, None), P("op"), P("sec"))
    return jax.shard_map(
        on_device, mesh=mesh, in_specs=placed, out_specs=P("sec", "op", None), check_vma=False
    )
```

```python
import jax
import jax.numpy as jnp
from jax import lax
from jax.experimental import pallas as pl
from jax.experimental.pallas import tpu as pltpu
from jax.sharding import PartitionSpec as P

NZ, NC, NY, NX = 4, 2, 4, 4
B = 256
OPS = 8
SECS = 16
QMAX = 2
HELD = SECS + 2 * QMAX
STRIP = OPS * 16
BF = jnp.bfloat16
F32 = jnp.float32


def flat(z, c, y, x):
    return ((z * NC + c) * NY + y) * NX + x


def move(block, target):
    route = []
    for z in range(NZ):
        for c in range(NC):
            for y in range(NY):
                for x in range(NX):
                    to = target(z, c, y, x)
                    if to is not None:
                        route.append((flat(z, c, y, x), flat(*to)))
    return lax.ppermute(block, ("op", "sec"), route)


def gather_first(d):
    def target(z, c, y, x):
        if c == 0:
            q = (y * NX + x + d) % SECS
            return (z, c, q // NX, q % NX)
        return (z, c, (y + d) % NY, x)

    return target


def gather_second(d):
    return lambda z, c, y, x: (z, c, (y + d) % NY, x) if c == 0 else (z, c, y, (x + d) % NX)


def to_core_1(z, c, y, x):
    return (z, 1, y, x) if c == 0 else None


def other_core(z, c, y, x):
    return (z, 1 - c, y, x)


def along_z(sign):
    return lambda z, c, y, x: ((z + (sign if c == 0 else -sign)) % NZ, c, y, x)


def masked(block, d):
    rows = lax.broadcasted_iota(jnp.int32, (B, B), 0)
    cols = lax.broadcasted_iota(jnp.int32, (B, B), 1)
    return jnp.where((rows < d) & (cols < d), block.astype(F32), 0.0).astype(BF)


def pack(dims_ref, first_psi, last_psi, left_ref, up_ref, down_ref):
    strip = left_ref[...].reshape(STRIP, B)
    up_ref[:STRIP, :] = strip
    down_ref[:STRIP, :] = strip
    for e in range(QMAX):
        to = slice(STRIP + e * B, STRIP + (e + 1) * B)
        up_ref[to, :] = masked(last_psi[e], dims_ref[SECS - QMAX + e])
        down_ref[to, :] = masked(first_psi[e], dims_ref[e])


def mask_sectors(dims_ref, psi_ref, masked_ref):
    def mask_one(s, _):
        masked_ref[s] = masked(psi_ref[s], dims_ref[s])
        return 0

    lax.fori_loop(0, SECS, mask_one, 0)


def unpack(place_ref, own, from_below, from_above, second_below, strips_ref, edges_ref):
    strips_ref[0] = own[...]
    strips_ref[1] = from_below[:STRIP, :].reshape(OPS, 16, B)
    strips_ref[2] = from_above[:STRIP, :].reshape(OPS, 16, B)
    strips_ref[3] = second_below[...]
    q = place_ref[2] * NX + place_ref[3]
    for k, (source, present) in enumerate(((from_below, q > 0), (from_above, q < SECS - 1))):
        keep = jnp.broadcast_to(present.astype(jnp.int32), (QMAX * B, B)) > 0
        edges_ref[k * QMAX * B:(k + 1) * QMAX * B, :] = jnp.where(keep, source[STRIP:, :].astype(F32), 0.0).astype(BF)


def by_twos(one):
    def two_operators(i, _):
        one(2 * i)
        one(2 * i + 1)
        return 0

    lax.fori_loop(0, OPS // 2, two_operators, 0)


def own_sectors(masked_ref, right_ref, h_ref):
    def one_operator(o):
        right_t = right_ref[o].T
        for s in range(0, SECS, 4):
            h = jnp.dot(masked_ref[s:s + 4].reshape(4 * B, B), right_t, preferred_element_type=F32)
            h_ref[o, (s + QMAX) * B:(s + QMAX + 4) * B, :] = h.astype(BF)

    by_twos(one_operator)


def edge_sectors(place_ref, edge_own, edge_other, right_ref, _, h_ref, edge_ref):
    core = place_ref[1]

    @pl.when(core == 0)
    def _():
        edge_ref[...] = edge_own[...]

    @pl.when(core == 1)
    def _():
        edge_ref[...] = edge_other[...]

    def one_operator(o):
        h = jnp.dot(edge_ref[...], right_ref[o].T, preferred_element_type=F32).astype(BF)
        h_ref[o, :QMAX * B, :] = h[:QMAX * B]
        h_ref[o, (SECS + QMAX) * B:, :] = h[QMAX * B:]

    by_twos(one_operator)


def second_product(shift_ref, place_ref, t0, t1, t2, t3, h_ref, mine_ref, other_ref, left_ref):
    z, core, y, x = place_ref[0], place_ref[1], place_ref[2], place_ref[3]
    for e, block in enumerate((t0, t1, t2, t3)):
        for d in range(4):
            step = (0, -1, 1, -2)[d]
            along_ring = (y * NX + x + step - e * NX + 2 * SECS) % SECS
            along_y = (y + step + NY) % NY * NX + (x - e + NX) % NX
            q = jnp.where(core == 0, along_ring, along_y)
            to_z, to_core = q // 4, (q // 2) % 2
            ahead = jnp.where(to_core == 0, to_z - z + NZ, z - to_z + NZ) % NZ
            start = jnp.where(to_core == core, 0, B // 2) + ahead * 32 + (q % 2) * 16
            start = pl.multiple_of(start, 16)
            for o in range(OPS):
                left_ref[pl.ds(start, 16), o * B:(o + 1) * B] = block[d, o]

    def four_targets(i, _):
        for u in range(4):
            t = i * 4 + u
            sources = [
                h_ref[o, pl.ds(pl.multiple_of((t + QMAX - shift_ref[o]) * B, B), B), :] for o in range(OPS)
            ]
            total = jnp.dot(left_ref[...], jnp.concatenate(sources, axis=0), preferred_element_type=F32)
            for k in range(NZ):
                mine_ref[k, t] = total[k * 32:(k + 1) * 32]
                other_ref[k, t] = total[B // 2 + k * 32:B // 2 + (k + 1) * 32].astype(BF)
        return 0

    lax.fori_loop(0, SECS // 4, four_targets, 0)


def on_device(psi, left_ops, right_ops, op_shift, sector_dims):
    p, q = lax.axis_index("op"), lax.axis_index("sec")
    core = p % NC
    place = jnp.stack([p // NC, core, q // NX, q % NX]).astype(jnp.int32)
    index = jnp.arange(B, dtype=jnp.int32)

    smem = pl.BlockSpec(memory_space=pltpu.SMEM)
    vmem = pl.BlockSpec(memory_space=pltpu.VMEM)

    def call(kernel, name, in_specs, out_shape, dots, scratch=(), aliases={}):
        return pl.pallas_call(
            kernel, in_specs=in_specs, out_shape=[jax.ShapeDtypeStruct(*o) for o in out_shape],
            out_specs=[vmem] * len(out_shape), name=name, scratch_shapes=scratch, input_output_aliases=aliases,
            compiler_params=pltpu.CompilerParams(vmem_limit_bytes=4 << 20),
            cost_estimate=pl.CostEstimate(flops=2 * dots * B ** 3, bytes_accessed=4 << 20, transcendentals=0))

    ends = pl.BlockSpec((QMAX, B, B), lambda i: (0, 0, 0)), pl.BlockSpec((QMAX, B, B), lambda i: (SECS // QMAX - 1, 0, 0))
    packed = jax.ShapeDtypeStruct((STRIP + QMAX * B, B), BF)
    whole = pl.BlockSpec((STRIP + QMAX * B, B), lambda i: (0, 0))
    psi_there = pltpu.with_memory_space_constraint(psi, pltpu.HBM)
    up, down = pl.pallas_call(
        pack, grid=(1,), in_specs=[smem, *ends, pl.BlockSpec((OPS, 16, B), lambda i: (0, 0, 0))],
        out_shape=[packed, packed], out_specs=[whole, whole], name="pack",
        compiler_params=pltpu.CompilerParams(vmem_limit_bytes=4 << 20),
        cost_estimate=pl.CostEstimate(flops=0, bytes_accessed=1 << 20, transcendentals=0),
    )(sector_dims, psi_there, psi_there, pltpu.with_memory_space_constraint(left_ops, pltpu.HBM))
    place, left_ops, up = lax.optimization_barrier((place, left_ops, up))
    up = move(up, gather_first(1))
    down = move(down, gather_first(-1))
    two = move(left_ops, gather_first(2))
    live_psi, = call(mask_sectors, "mask_sectors", [smem, vmem], [((SECS, B, B), BF)], 0)(sector_dims, psi)
    two, _ = lax.optimization_barrier((two, live_psi))
    strips, edges = call(
        unpack, "unpack", [smem] + [vmem] * 4, [((4, OPS, 16, B), BF), ((2 * QMAX * B, B), BF)], 0,
    )(place, left_ops, up, down, two)
    seconds = [move(strips, gather_second(d)) for d in (1, 3, 2)]
    t0, t1, t3, t2 = strips, *seconds
    edges_other = move(edges, to_core_1)

    live_psi, _ = lax.optimization_barrier((live_psi, edges))
    h, = call(
        own_sectors, "own_sectors", [vmem] * 2, [((OPS, HELD * B, B), BF)], OPS * SECS,
    )(live_psi, right_ops)
    h, = call(
        edge_sectors, "edge_sectors", [smem] + [vmem] * 4, [((OPS, HELD * B, B), BF)], 1,
        [pltpu.VMEM((2 * QMAX * B, B), BF)], {4: 0},
    )(place, edges, edges_other, right_ops, h)
    mine, other = call(
        second_product, "second_product", [smem, smem] + [vmem] * 5,
        [((NZ, SECS, 32, B), F32), ((NZ, SECS, 32, B), BF)], OPS * SECS, [pltpu.VMEM((B, OPS * B), BF)],
    )(op_shift, place, t0, t1, t2, t3, h)

    total = mine + move(other, other_core).astype(F32)
    far = move(total[2].astype(BF), along_z(1))
    back = move(total[3].astype(BF), along_z(-1))
    near = move((total[1] + far.astype(F32)).astype(BF), along_z(1))
    summed = total[0] + back.astype(F32) + near.astype(F32)
    live = index[None, :] < sector_dims[:, None]
    mine_rows = p * 32 + jnp.arange(32, dtype=jnp.int32)
    live_rows = mine_rows[None, :] < sector_dims[:, None]
    return jnp.where(live_rows[:, :, None] & live[:, None, :], summed, 0.0).astype(BF)


def solution(mesh):
    placed = (P("sec", None, None), P("op", "sec", None), P("op", None, None), P("op"), P("sec"))
    return jax.shard_map(
        on_device, mesh=mesh, in_specs=placed, out_specs=P("sec", "op", None), check_vma=False
    )
```

```python
import functools

import jax
import jax.numpy as jnp
from jax import lax
from jax.experimental import pallas as pl
from jax.experimental.pallas import tpu as pltpu
from jax.sharding import PartitionSpec as P

NZ, NC, NY, NX = 4, 2, 4, 4
B = 256
OPS = 8
SECS = 16
QMAX = 2
HELD = SECS + 2 * QMAX
STRIP = OPS * 16
EARLY = 4
SPLIT = 12
BF = jnp.bfloat16
F32 = jnp.float32


def flat(z, c, y, x):
    return ((z * NC + c) * NY + y) * NX + x


def move(block, target):
    route = []
    for z in range(NZ):
        for c in range(NC):
            for y in range(NY):
                for x in range(NX):
                    to = target(z, c, y, x)
                    if to is not None:
                        route.append((flat(z, c, y, x), flat(*to)))
    return lax.ppermute(block, ("op", "sec"), route)


def gather_first(d):
    def target(z, c, y, x):
        if c == 0:
            q = (y * NX + x + d) % SECS
            return (z, c, q // NX, q % NX)
        return (z, c, (y + d) % NY, x)

    return target


def gather_second(d):
    return lambda z, c, y, x: (z, c, (y + d) % NY, x) if c == 0 else (z, c, y, (x + d) % NX)


def other_core(z, c, y, x):
    return (z, 1 - c, y, x)


def along_z(sign):
    return lambda z, c, y, x: ((z + (sign if c == 0 else -sign)) % NZ, c, y, x)


def masked(block, d):
    rows = lax.broadcasted_iota(jnp.int32, (B, B), 0)
    cols = lax.broadcasted_iota(jnp.int32, (B, B), 1)
    return jnp.where((rows < d) & (cols < d), block.astype(F32), 0.0).astype(BF)


def pack(dims_ref, first_psi, last_psi, left_ref, up_ref, down_ref):
    strip = left_ref[...].reshape(STRIP, B)
    up_ref[:STRIP, :] = strip
    down_ref[:STRIP, :] = strip
    for e in range(QMAX):
        to = slice(STRIP + e * B, STRIP + (e + 1) * B)
        up_ref[to, :] = masked(last_psi[e], dims_ref[SECS - QMAX + e])
        down_ref[to, :] = masked(first_psi[e], dims_ref[e])


def unpack(place_ref, own, from_below, from_above, second_below, after, strips_ref, edges_ref):
    strips_ref[0] = own[:STRIP, :].reshape(OPS, 16, B)
    strips_ref[1] = from_below[:STRIP, :].reshape(OPS, 16, B)
    strips_ref[2] = from_above[:STRIP, :].reshape(OPS, 16, B)
    strips_ref[3] = second_below[...]
    q = place_ref[2] * NX + place_ref[3]
    for k, (source, present) in enumerate(((from_below, q > 0), (from_above, q < SECS - 1))):
        keep = jnp.broadcast_to(present.astype(jnp.int32), (QMAX * B, B)) > 0
        edges_ref[k * QMAX * B:(k + 1) * QMAX * B, :] = jnp.where(keep, source[STRIP:, :].astype(F32), 0.0).astype(BF)


def by_twos(one, ops=(0, OPS)):
    def two_operators(i, _):
        one(2 * i)
        one(2 * i + 1)
        return 0

    lax.fori_loop(ops[0] // 2, ops[1] // 2, two_operators, 0)


def own_sectors(ops, masked_ref, right_ref, *refs):
    h_ref = refs[-1]

    def one_operator(o):
        right_t = right_ref[o].T
        for s in range(0, SECS, 4):
            h = jnp.dot(masked_ref[s:s + 4].reshape(4 * B, B), right_t, preferred_element_type=F32)
            h_ref[o, (s + QMAX) * B:(s + QMAX + 4) * B, :] = h.astype(BF)

    by_twos(one_operator, ops)


def first_operators(dims_ref, psi_hbm, right_hbm, masked_ref, right_ref, h_ref, done_ref, psi_sem, right_sem):
    right_in = pltpu.make_async_copy(right_hbm, right_ref, right_sem)

    def psi_in(s):
        return pltpu.make_async_copy(psi_hbm.at[s], masked_ref.at[s], psi_sem.at[s])

    for s in range(SECS):
        psi_in(s).start()
    right_in.start()

    def mask_one(s, _):
        psi_in(s).wait()
        masked_ref[s] = masked(masked_ref[s], dims_ref[s])
        return 0

    lax.fori_loop(0, SECS, mask_one, 0)
    right_in.wait()
    own_sectors((0, EARLY), masked_ref, right_ref, h_ref)
    done_ref[...] = jnp.zeros_like(done_ref)


def edge_sectors(place_ref, edge_own, edge_other, right_ref, _, h_ref, edge_ref):
    core = place_ref[1]

    @pl.when(core == 0)
    def _():
        edge_ref[...] = edge_own[...]

    @pl.when(core == 1)
    def _():
        edge_ref[...] = edge_other[...]

    def one_operator(o):
        h = jnp.dot(edge_ref[...], right_ref[o].T, preferred_element_type=F32).astype(BF)
        h_ref[o, :QMAX * B, :] = h[:QMAX * B]
        h_ref[o, (SECS + QMAX) * B:, :] = h[QMAX * B:]

    by_twos(one_operator)


def order_left(place_ref, t0, t1, t2, t3, left_ref):
    z, core, y, x = place_ref[0], place_ref[1], place_ref[2], place_ref[3]
    for e, block in enumerate((t0, t1, t2, t3)):
        for d in range(4):
            step = (0, -1, 1, -2)[d]
            along_ring = (y * NX + x + step - e * NX + 2 * SECS) % SECS
            along_y = (y + step + NY) % NY * NX + (x - e + NX) % NX
            q = jnp.where(core == 0, along_ring, along_y)
            to_z, to_core = q // 4, (q // 2) % 2
            ahead = jnp.where(to_core == 0, to_z - z + NZ, z - to_z + NZ) % NZ
            start = jnp.where(to_core == core, 0, B // 2) + ahead * 32 + (q % 2) * 16
            start = pl.multiple_of(start, 16)
            for o in range(OPS):
                left_ref[pl.ds(start, 16), o * B:(o + 1) * B] = block[d, o]


def some_targets(first, shift_ref, left_ref, h_ref, mine_ref, other_ref):
    def four_targets(i, _):
        for u in range(4):
            t = i * 4 + u
            sources = [
                h_ref[o, pl.ds(pl.multiple_of((first + t + QMAX - shift_ref[o]) * B, B), B), :] for o in range(OPS)
            ]
            total = jnp.dot(left_ref[...], jnp.concatenate(sources, axis=0), preferred_element_type=F32)
            for k in range(NZ):
                mine_ref[k, t] = total[k * 32:(k + 1) * 32]
                other_ref[k, t] = total[B // 2 + k * 32:B // 2 + (k + 1) * 32].astype(BF)
        return 0

    lax.fori_loop(0, mine_ref.shape[1] // 4, four_targets, 0)


def first_targets(shift_ref, place_ref, t0, t1, t2, t3, h_ref, mine_ref, other_ref, left_ref):
    order_left(place_ref, t0, t1, t2, t3, left_ref)
    some_targets(0, shift_ref, left_ref, h_ref, mine_ref, other_ref)


def add_cores(mine_a, mine_b, got_a, got_b, own_ref, near_ref, far_ref, back_ref):
    for mine, got, to in ((mine_a, got_a, slice(0, SPLIT)), (mine_b, got_b, slice(SPLIT, SECS))):
        own_ref[to] = mine[0] + got[0].astype(F32)
        near_ref[to] = mine[1] + got[1].astype(F32)
        far_ref[to] = (mine[2] + got[2].astype(F32)).astype(BF)
        back_ref[to] = (mine[3] + got[3].astype(F32)).astype(BF)


def on_device(psi, left_ops, right_ops, op_shift, sector_dims):
    p, q = lax.axis_index("op"), lax.axis_index("sec")
    core = p % NC
    place = jnp.stack([p // NC, core, q // NX, q % NX]).astype(jnp.int32)

    smem = pl.BlockSpec(memory_space=pltpu.SMEM)
    vmem = pl.BlockSpec(memory_space=pltpu.VMEM)
    hbm = pl.BlockSpec(memory_space=pltpu.HBM)

    def call(kernel, name, in_specs, out_shape, dots, scratch=(), aliases={}):
        return pl.pallas_call(
            kernel, in_specs=in_specs, out_shape=[jax.ShapeDtypeStruct(*o) for o in out_shape],
            out_specs=[vmem] * len(out_shape), name=name, scratch_shapes=scratch, input_output_aliases=aliases,
            compiler_params=pltpu.CompilerParams(vmem_limit_bytes=4 << 20),
            cost_estimate=pl.CostEstimate(flops=2 * dots * B ** 3, bytes_accessed=(4 << 20) * (dots > 0), transcendentals=0))

    ends = pl.BlockSpec((QMAX, B, B), lambda i: (0, 0, 0)), pl.BlockSpec((QMAX, B, B), lambda i: (SECS // QMAX - 1, 0, 0))
    packed = jax.ShapeDtypeStruct((STRIP + QMAX * B, B), BF)
    whole = pl.BlockSpec((STRIP + QMAX * B, B), lambda i: (0, 0))
    dims_there = pltpu.with_memory_space_constraint(sector_dims, pltpu.HBM)
    right_there = pltpu.with_memory_space_constraint(right_ops, pltpu.HBM)
    psi_there = pltpu.with_memory_space_constraint(psi, pltpu.HBM)
    up, down = pl.pallas_call(
        pack, grid=(1,), in_specs=[smem, *ends, pl.BlockSpec((OPS, 16, B), lambda i: (0, 0, 0))],
        out_shape=[packed, packed], out_specs=[whole, whole], name="pack",
        compiler_params=pltpu.CompilerParams(vmem_limit_bytes=4 << 20),
        cost_estimate=pl.CostEstimate(flops=0, bytes_accessed=1 << 20, transcendentals=0),
    )(dims_there, psi_there, psi_there, pltpu.with_memory_space_constraint(left_ops, pltpu.HBM))
    place, left_ops, up = lax.optimization_barrier((place, left_ops, up))
    sent = up
    up = move(sent, gather_first(1))
    down = move(down, gather_first(-1))
    two = move(left_ops, gather_first(2))
    live_psi, right, h, done = call(
        first_operators, "first_operators", [smem, hbm, hbm],
        [((SECS, B, B), BF), ((OPS, B, B), BF), ((OPS, HELD * B, B), BF), ((8, 128), F32)], EARLY * SECS,
        [pltpu.SemaphoreType.DMA((SECS,)), pltpu.SemaphoreType.DMA],
    )(dims_there, psi_there, right_there)
    strips, edges = call(
        unpack, "unpack", [smem] + [vmem] * 5, [((4, OPS, 16, B), BF), ((2 * QMAX * B, B), BF)], 0,
    )(place, sent, up, down, two, done)
    seconds = [move(strips, gather_second(d)) for d in (1, 3, 2)]
    t0, t1, t3, t2 = strips, *seconds
    edges_other = move(edges, other_core)

    h, = call(
        functools.partial(own_sectors, (EARLY, OPS)), "own_sectors", [vmem] * 4, [((OPS, HELD * B, B), BF)],
        0, (), {3: 0},
    )(live_psi, right, strips, h)
    h, = call(
        edge_sectors, "edge_sectors", [smem] + [vmem] * 4, [((OPS, HELD * B, B), BF)], 0,
        [pltpu.VMEM((2 * QMAX * B, B), BF)], {4: 0},
    )(place, edges, edges_other, right, h)
    first_a = [((NZ, SPLIT, 32, B), F32), ((NZ, SPLIT, 32, B), BF), ((B, OPS * B), BF)]
    mine_a, away_a, left = call(first_targets, "first_targets", [smem, smem] + [vmem] * 5, first_a, OPS * SPLIT)(
        op_shift, place, t0, t1, t2, t3, h)
    rest = [((NZ, SECS - SPLIT, 32, B), F32), ((NZ, SECS - SPLIT, 32, B), BF)]
    mine_b, away_b = call(
        functools.partial(some_targets, SPLIT), "last_targets", [smem, vmem, vmem], rest, OPS * (SECS - SPLIT),
    )(op_shift, left, h)

    slot = (SECS, 32, B)
    own, near, far, back = call(
        add_cores, "add_cores", [vmem] * 4, [(slot, F32), (slot, F32), (slot, BF), (slot, BF)], 0,
    )(mine_a, mine_b, move(away_a, other_core), move(away_b, other_core))
    far = move(far, along_z(1))
    back = move(back, along_z(-1))
    near = move((near + far.astype(F32)).astype(BF), along_z(1))
    summed = own + back.astype(F32) + near.astype(F32)
    index = jnp.arange(B, dtype=jnp.int32)
    live = index[None, :] < sector_dims[:, None]
    mine_rows = p * 32 + jnp.arange(32, dtype=jnp.int32)
    live_rows = mine_rows[None, :] < sector_dims[:, None]
    return jnp.where(live_rows[:, :, None] & live[:, None, :], summed, 0.0).astype(BF)


def solution(mesh):
    placed = (P("sec", None, None), P("op", "sec", None), P("op", None, None), P("op"), P("sec"))
    return jax.shard_map(
        on_device, mesh=mesh, in_specs=placed, out_specs=P("sec", "op", None), check_vma=False
    )
```

```python
import functools

import jax
import jax.numpy as jnp
from jax import lax
from jax.experimental import pallas as pl
from jax.experimental.pallas import tpu as pltpu
from jax.sharding import PartitionSpec as P

NZ, NC, NY, NX = 4, 2, 4, 4
B = 256
OPS = 8
SECS = 16
QMAX = 2
HELD = SECS + 2 * QMAX
STRIP = OPS * 16
EARLY = 4
SPLIT = 12
BF = jnp.bfloat16
F32 = jnp.float32


def flat(z, c, y, x):
    return ((z * NC + c) * NY + y) * NX + x


def move(block, target):
    route = []
    for z in range(NZ):
        for c in range(NC):
            for y in range(NY):
                for x in range(NX):
                    to = target(z, c, y, x)
                    if to is not None:
                        route.append((flat(z, c, y, x), flat(*to)))
    return lax.ppermute(block, ("op", "sec"), route)


def gather_first(d):
    def target(z, c, y, x):
        if c == 0:
            q = (y * NX + x + d) % SECS
            return (z, c, q // NX, q % NX)
        return (z, c, (y + d) % NY, x)

    return target


def gather_second(d):
    return lambda z, c, y, x: (z, c, (y + d) % NY, x) if c == 0 else (z, c, y, (x + d) % NX)


def other_core(z, c, y, x):
    return (z, 1 - c, y, x)


def along_z(sign):
    return lambda z, c, y, x: ((z + (sign if c == 0 else -sign)) % NZ, c, y, x)


def masked(block, d):
    rows = lax.broadcasted_iota(jnp.int32, (B, B), 0)
    cols = lax.broadcasted_iota(jnp.int32, (B, B), 1)
    return jnp.where((rows < d) & (cols < d), block.astype(F32), 0.0).astype(BF)


def pack(dims_ref, first_psi, last_psi, left_ref, up_ref, down_ref):
    strip = left_ref[...].reshape(STRIP, B)
    up_ref[:STRIP, :] = strip
    down_ref[:STRIP, :] = strip
    for e in range(QMAX):
        to = slice(STRIP + e * B, STRIP + (e + 1) * B)
        up_ref[to, :] = masked(last_psi[e], dims_ref[SECS - QMAX + e])
        down_ref[to, :] = masked(first_psi[e], dims_ref[e])


def unpack(place_ref, own, from_below, from_above, second_below, after, strips_ref, edges_ref):
    strips_ref[0] = own[:STRIP, :].reshape(OPS, 16, B)
    strips_ref[1] = from_below[:STRIP, :].reshape(OPS, 16, B)
    strips_ref[2] = from_above[:STRIP, :].reshape(OPS, 16, B)
    strips_ref[3] = second_below[...]
    q = place_ref[2] * NX + place_ref[3]
    for k, (source, present) in enumerate(((from_below, q > 0), (from_above, q < SECS - 1))):
        keep = jnp.broadcast_to(present.astype(jnp.int32), (QMAX * B, B)) > 0
        edges_ref[k * QMAX * B:(k + 1) * QMAX * B, :] = jnp.where(keep, source[STRIP:, :].astype(F32), 0.0).astype(BF)


def by_twos(one, ops=(0, OPS)):
    def two_operators(i, _):
        one(2 * i)
        one(2 * i + 1)
        return 0

    lax.fori_loop(ops[0] // 2, ops[1] // 2, two_operators, 0)


def own_sectors(ops, masked_ref, right_ref, *refs):
    h_ref = refs[-1]

    def one_operator(o):
        right_t = right_ref[o].T
        for s in range(0, SECS, 4):
            h = jnp.dot(masked_ref[s:s + 4].reshape(4 * B, B), right_t, preferred_element_type=F32)
            h_ref[o, (s + QMAX) * B:(s + QMAX + 4) * B, :] = h.astype(BF)

    by_twos(one_operator, ops)


def first_operators(dims_ref, psi_hbm, right_hbm, masked_ref, right_ref, h_ref, done_ref, psi_sem, right_sem):
    right_in = pltpu.make_async_copy(right_hbm, right_ref, right_sem)

    def psi_in(s):
        return pltpu.make_async_copy(psi_hbm.at[s], masked_ref.at[s], psi_sem.at[s])

    for s in range(SECS):
        psi_in(s).start()
    right_in.start()

    def mask_one(s, _):
        psi_in(s).wait()
        masked_ref[s] = masked(masked_ref[s], dims_ref[s])
        return 0

    lax.fori_loop(0, SECS, mask_one, 0)
    right_in.wait()
    own_sectors((0, EARLY), masked_ref, right_ref, h_ref)
    done_ref[...] = jnp.zeros_like(done_ref)


def other_sectors(shift_ref, place_ref, edge_own, edge_other, masked_ref, right_ref, _, h_ref, edge_ref):
    core = place_ref[1]

    @pl.when(core == 0)
    def _():
        edge_ref[...] = edge_own[...]

    @pl.when(core == 1)
    def _():
        edge_ref[...] = edge_other[...]

    def edge_side(o):
        above = (shift_ref[o] < 0).astype(jnp.int32)
        source = pl.multiple_of(above * (QMAX * B), QMAX * B)
        to = pl.multiple_of(above * ((QMAX + SECS) * B), QMAX * B)
        h = jnp.dot(edge_ref[pl.ds(source, QMAX * B), :], right_ref[o].T, preferred_element_type=F32)
        h_ref[o, pl.ds(to, QMAX * B), :] = h.astype(BF)

    own_sectors((EARLY, OPS), masked_ref, right_ref, h_ref)
    for o in range(OPS):
        edge_side(o)


def order_left(place_ref, t0, t1, t2, t3, left_ref):
    z, core, y, x = place_ref[0], place_ref[1], place_ref[2], place_ref[3]
    for e, block in enumerate((t0, t1, t2, t3)):
        for d in range(4):
            step = (0, -1, 1, -2)[d]
            along_ring = (y * NX + x + step - e * NX + 2 * SECS) % SECS
            along_y = (y + step + NY) % NY * NX + (x - e + NX) % NX
            q = jnp.where(core == 0, along_ring, along_y)
            to_z, to_core = q // 4, (q // 2) % 2
            ahead = jnp.where(to_core == 0, to_z - z + NZ, z - to_z + NZ) % NZ
            start = jnp.where(to_core == core, 0, B // 2) + ahead * 32 + (q % 2) * 16
            start = pl.multiple_of(start, 16)
            for o in range(OPS):
                left_ref[pl.ds(start, 16), o * B:(o + 1) * B] = block[d, o]


def some_targets(first, shift_ref, left_ref, h_ref, mine_ref, other_ref):
    def four_targets(i, _):
        for u in range(4):
            t = i * 4 + u
            sources = [
                h_ref[o, pl.ds(pl.multiple_of((first + t + QMAX - shift_ref[o]) * B, B), B), :] for o in range(OPS)
            ]
            total = jnp.dot(left_ref[...], jnp.concatenate(sources, axis=0), preferred_element_type=F32)
            for k in range(NZ):
                mine_ref[k, t] = total[k * 32:(k + 1) * 32]
                other_ref[k, t] = total[B // 2 + k * 32:B // 2 + (k + 1) * 32].astype(BF)
        return 0

    lax.fori_loop(0, mine_ref.shape[1] // 4, four_targets, 0)


def first_targets(shift_ref, place_ref, t0, t1, t2, t3, h_ref, mine_ref, other_ref, left_ref):
    order_left(place_ref, t0, t1, t2, t3, left_ref)
    some_targets(0, shift_ref, left_ref, h_ref, mine_ref, other_ref)


def add_cores(mine_a, mine_b, got_a, got_b, own_ref, near_ref, far_ref, back_ref):
    for mine, got, to in ((mine_a, got_a, slice(0, SPLIT)), (mine_b, got_b, slice(SPLIT, SECS))):
        own_ref[to] = mine[0] + got[0].astype(F32)
        near_ref[to] = mine[1] + got[1].astype(F32)
        far_ref[to] = (mine[2] + got[2].astype(F32)).astype(BF)
        back_ref[to] = (mine[3] + got[3].astype(F32)).astype(BF)


def on_device(psi, left_ops, right_ops, op_shift, sector_dims):
    p, q = lax.axis_index("op"), lax.axis_index("sec")
    core = p % NC
    place = jnp.stack([p // NC, core, q // NX, q % NX]).astype(jnp.int32)

    smem = pl.BlockSpec(memory_space=pltpu.SMEM)
    vmem = pl.BlockSpec(memory_space=pltpu.VMEM)
    hbm = pl.BlockSpec(memory_space=pltpu.HBM)

    def call(kernel, name, in_specs, out_shape, dots, scratch=(), aliases={}):
        return pl.pallas_call(
            kernel, in_specs=in_specs, out_shape=[jax.ShapeDtypeStruct(*o) for o in out_shape],
            out_specs=[vmem] * len(out_shape), name=name, scratch_shapes=scratch, input_output_aliases=aliases,
            compiler_params=pltpu.CompilerParams(vmem_limit_bytes=4 << 20),
            cost_estimate=pl.CostEstimate(flops=2 * dots * B ** 3, bytes_accessed=(4 << 20) * (dots > 0), transcendentals=0))

    ends = pl.BlockSpec((QMAX, B, B), lambda i: (0, 0, 0)), pl.BlockSpec((QMAX, B, B), lambda i: (SECS // QMAX - 1, 0, 0))
    packed = jax.ShapeDtypeStruct((STRIP + QMAX * B, B), BF)
    whole = pl.BlockSpec((STRIP + QMAX * B, B), lambda i: (0, 0))
    dims_there = pltpu.with_memory_space_constraint(sector_dims, pltpu.HBM)
    right_there = pltpu.with_memory_space_constraint(right_ops, pltpu.HBM)
    psi_there = pltpu.with_memory_space_constraint(psi, pltpu.HBM)
    up, down = pl.pallas_call(
        pack, grid=(1,), in_specs=[smem, *ends, pl.BlockSpec((OPS, 16, B), lambda i: (0, 0, 0))],
        out_shape=[packed, packed], out_specs=[whole, whole], name="pack",
        compiler_params=pltpu.CompilerParams(vmem_limit_bytes=4 << 20),
        cost_estimate=pl.CostEstimate(flops=0, bytes_accessed=1 << 20, transcendentals=0),
    )(dims_there, psi_there, psi_there, pltpu.with_memory_space_constraint(left_ops, pltpu.HBM))
    place, left_ops, up = lax.optimization_barrier((place, left_ops, up))
    sent = up
    up = move(sent, gather_first(1))
    down = move(down, gather_first(-1))
    two = move(left_ops, gather_first(2))
    live_psi, right, h, done = call(
        first_operators, "first_operators", [smem, hbm, hbm],
        [((SECS, B, B), BF), ((OPS, B, B), BF), ((OPS, HELD * B, B), BF), ((8, 128), F32)], EARLY * SECS,
        [pltpu.SemaphoreType.DMA((SECS,)), pltpu.SemaphoreType.DMA],
    )(dims_there, psi_there, right_there)
    strips, edges = call(
        unpack, "unpack", [smem] + [vmem] * 5, [((4, OPS, 16, B), BF), ((2 * QMAX * B, B), BF)], 0,
    )(place, sent, up, down, two, done)
    seconds = [move(strips, gather_second(d)) for d in (1, 3, 2)]
    t0, t1, t3, t2 = strips, *seconds
    edges_other = move(edges, other_core)

    h, = call(
        other_sectors, "other_sectors", [smem, smem] + [vmem] * 5, [((OPS, HELD * B, B), BF)], 0,
        [pltpu.VMEM((2 * QMAX * B, B), BF)], {6: 0},
    )(op_shift, place, edges, edges_other, live_psi, right, h)

    first_a = [((NZ, SPLIT, 32, B), F32), ((NZ, SPLIT, 32, B), BF), ((B, OPS * B), BF)]
    mine_a, away_a, left = call(first_targets, "first_targets", [smem, smem] + [vmem] * 5, first_a, OPS * SPLIT)(
        op_shift, place, t0, t1, t2, t3, h)
    rest = [((NZ, SECS - SPLIT, 32, B), F32), ((NZ, SECS - SPLIT, 32, B), BF)]
    mine_b, away_b = call(
        functools.partial(some_targets, SPLIT), "last_targets", [smem, vmem, vmem], rest, OPS * (SECS - SPLIT),
    )(op_shift, left, h)

    slot = (SECS, 32, B)
    own, near, far, back = call(
        add_cores, "add_cores", [vmem] * 4, [(slot, F32), (slot, F32), (slot, BF), (slot, BF)], 0,
    )(mine_a, mine_b, move(away_a, other_core), move(away_b, other_core))
    far = move(far, along_z(1))
    back = move(back, along_z(-1))
    near = move((near + far.astype(F32)).astype(BF), along_z(1))
    summed = own + back.astype(F32) + near.astype(F32)
    index = jnp.arange(B, dtype=jnp.int32)
    live = index[None, :] < sector_dims[:, None]
    mine_rows = p * 32 + jnp.arange(32, dtype=jnp.int32)
    live_rows = mine_rows[None, :] < sector_dims[:, None]
    return jnp.where(live_rows[:, :, None] & live[:, None, :], summed, 0.0).astype(BF)


def solution(mesh):
    placed = (P("sec", None, None), P("op", "sec", None), P("op", None, None), P("op"), P("sec"))
    return jax.shard_map(
        on_device, mesh=mesh, in_specs=placed, out_specs=P("sec", "op", None), check_vma=False
    )
```

```python
import functools

import jax
import jax.numpy as jnp
from jax import lax
from jax.experimental import pallas as pl
from jax.experimental.pallas import tpu as pltpu
from jax.sharding import PartitionSpec as P

NZ, NC, NY, NX = 4, 2, 4, 4
B = 256
OPS = 8
SECS = 16
QMAX = 2
HELD = SECS + 2 * QMAX
STRIP = OPS * 16
EARLY = 4
SPLIT = 12
BF = jnp.bfloat16
F32 = jnp.float32


def flat(z, c, y, x):
    return ((z * NC + c) * NY + y) * NX + x


def move(block, target):
    route = []
    for z in range(NZ):
        for c in range(NC):
            for y in range(NY):
                for x in range(NX):
                    to = target(z, c, y, x)
                    if to is not None:
                        route.append((flat(z, c, y, x), flat(*to)))
    return lax.ppermute(block, ("op", "sec"), route)


def gather_first(d):
    def target(z, c, y, x):
        if c == 0:
            q = (y * NX + x + d) % SECS
            return (z, c, q // NX, q % NX)
        return (z, c, (y + d) % NY, x)

    return target


def gather_second(d):
    return lambda z, c, y, x: (z, c, (y + d) % NY, x) if c == 0 else (z, c, y, (x + d) % NX)


def other_core(z, c, y, x):
    return (z, 1 - c, y, x)


def along_z(sign):
    return lambda z, c, y, x: ((z + (sign if c == 0 else -sign)) % NZ, c, y, x)


def masked(block, d):
    rows = lax.broadcasted_iota(jnp.int32, (B, B), 0)
    cols = lax.broadcasted_iota(jnp.int32, (B, B), 1)
    return jnp.where((rows < d) & (cols < d), block.astype(F32), 0.0).astype(BF)


def pack(dims_ref, first_psi, last_psi, left_ref, up_ref, down_ref):
    strip = left_ref[...].reshape(STRIP, B)
    up_ref[:STRIP, :] = strip
    down_ref[:STRIP, :] = strip
    for e in range(QMAX):
        to = slice(STRIP + e * B, STRIP + (e + 1) * B)
        up_ref[to, :] = masked(last_psi[e], dims_ref[SECS - QMAX + e])
        down_ref[to, :] = masked(first_psi[e], dims_ref[e])


def unpack(own, from_below, from_above, second_below, after, strips_ref):
    strips_ref[0] = own[:STRIP, :].reshape(OPS, 16, B)
    strips_ref[1] = from_below[:STRIP, :].reshape(OPS, 16, B)
    strips_ref[2] = from_above[:STRIP, :].reshape(OPS, 16, B)
    strips_ref[3] = second_below[...]


def by_twos(one, ops=(0, OPS)):
    def two_operators(i, _):
        one(2 * i)
        one(2 * i + 1)
        return 0

    lax.fori_loop(ops[0] // 2, ops[1] // 2, two_operators, 0)


def own_sectors(ops, masked_ref, right_ref, *refs):
    h_ref = refs[-1]

    def one_operator(o):
        right_t = right_ref[o].T
        for s in range(0, SECS, 4):
            h = jnp.dot(masked_ref[s:s + 4].reshape(4 * B, B), right_t, preferred_element_type=F32)
            h_ref[o, (s + QMAX) * B:(s + QMAX + 4) * B, :] = h.astype(BF)

    by_twos(one_operator, ops)


def first_operators(dims_ref, psi_hbm, right_hbm, masked_ref, right_ref, h_ref, done_ref, psi_sem, right_sem):
    right_in = pltpu.make_async_copy(right_hbm, right_ref, right_sem)

    def psi_in(s):
        return pltpu.make_async_copy(psi_hbm.at[s], masked_ref.at[s], psi_sem.at[s])

    for s in range(SECS):
        psi_in(s).start()
    right_in.start()

    def mask_one(s, _):
        psi_in(s).wait()
        masked_ref[s] = masked(masked_ref[s], dims_ref[s])
        return 0

    lax.fori_loop(0, SECS, mask_one, 0)
    right_in.wait()
    own_sectors((0, EARLY), masked_ref, right_ref, h_ref)
    done_ref[...] = jnp.zeros_like(done_ref)


def other_sectors(shift_ref, place_ref, below_0, above_0, below_1, above_1, masked_ref, right_ref, _, h_ref, edge_ref):
    core = place_ref[1]
    q = place_ref[2] * NX + place_ref[3]
    for k, (sources, present) in enumerate((((below_0, below_1), q > 0), ((above_0, above_1), q < SECS - 1))):
        to = slice(k * QMAX * B, (k + 1) * QMAX * B)
        for c, source in enumerate(sources):

            @pl.when(present & (core == c))
            def _():
                edge_ref[to, :] = source[STRIP:, :]

        @pl.when(jnp.logical_not(present))
        def _():
            edge_ref[to, :] = jnp.zeros((QMAX * B, B), BF)

    def edge_side(o):
        above = (shift_ref[o] < 0).astype(jnp.int32)
        source = pl.multiple_of(above * (QMAX * B), QMAX * B)
        to = pl.multiple_of(above * ((QMAX + SECS) * B), QMAX * B)
        h = jnp.dot(edge_ref[pl.ds(source, QMAX * B), :], right_ref[o].T, preferred_element_type=F32)
        h_ref[o, pl.ds(to, QMAX * B), :] = h.astype(BF)

    own_sectors((EARLY, OPS), masked_ref, right_ref, h_ref)
    for o in range(OPS):
        edge_side(o)


def order_left(place_ref, t0, t1, t2, t3, left_ref):
    z, core, y, x = place_ref[0], place_ref[1], place_ref[2], place_ref[3]
    for e, block in enumerate((t0, t1, t2, t3)):
        for d in range(4):
            step = (0, -1, 1, -2)[d]
            along_ring = (y * NX + x + step - e * NX + 2 * SECS) % SECS
            along_y = (y + step + NY) % NY * NX + (x - e + NX) % NX
            q = jnp.where(core == 0, along_ring, along_y)
            to_z, to_core = q // 4, (q // 2) % 2
            ahead = jnp.where(to_core == 0, to_z - z + NZ, z - to_z + NZ) % NZ
            start = jnp.where(to_core == core, 0, B // 2) + ahead * 32 + (q % 2) * 16
            start = pl.multiple_of(start, 16)
            for o in range(OPS):
                left_ref[pl.ds(start, 16), o * B:(o + 1) * B] = block[d, o]


def some_targets(first, shift_ref, left_ref, h_ref, mine_ref, other_ref):
    count = mine_ref.shape[1]
    at_once = min(count, 6)

    def several_targets(i, _):
        for u in range(at_once):
            t = i * at_once + u
            sources = [
                h_ref[o, pl.ds(pl.multiple_of((first + t + QMAX - shift_ref[o]) * B, B), B), :] for o in range(OPS)
            ]
            total = jnp.dot(left_ref[...], jnp.concatenate(sources, axis=0), preferred_element_type=F32)
            for k in range(NZ):
                mine_ref[k, t] = total[k * 32:(k + 1) * 32]
                other_ref[k, t] = total[B // 2 + k * 32:B // 2 + (k + 1) * 32].astype(BF)
        return 0

    lax.fori_loop(0, count // at_once, several_targets, 0)


def first_targets(shift_ref, place_ref, t0, t1, t2, t3, h_ref, mine_ref, other_ref, left_ref):
    order_left(place_ref, t0, t1, t2, t3, left_ref)
    some_targets(0, shift_ref, left_ref, h_ref, mine_ref, other_ref)


def add_cores(mine_a, mine_b, got_a, got_b, own_ref, near_ref, far_ref, back_ref):
    for mine, got, to in ((mine_a, got_a, slice(0, SPLIT)), (mine_b, got_b, slice(SPLIT, SECS))):
        own_ref[to] = mine[0] + got[0].astype(F32)
        near_ref[to] = mine[1] + got[1].astype(F32)
        far_ref[to] = (mine[2] + got[2].astype(F32)).astype(BF)
        back_ref[to] = (mine[3] + got[3].astype(F32)).astype(BF)


def on_device(psi, left_ops, right_ops, op_shift, sector_dims):
    p, q = lax.axis_index("op"), lax.axis_index("sec")
    core = p % NC
    place = jnp.stack([p // NC, core, q // NX, q % NX]).astype(jnp.int32)

    smem = pl.BlockSpec(memory_space=pltpu.SMEM)
    vmem = pl.BlockSpec(memory_space=pltpu.VMEM)
    hbm = pl.BlockSpec(memory_space=pltpu.HBM)

    def call(kernel, name, in_specs, out_shape, dots, scratch=(), aliases={}):
        return pl.pallas_call(
            kernel, in_specs=in_specs, out_shape=[jax.ShapeDtypeStruct(*o) for o in out_shape],
            out_specs=[vmem] * len(out_shape), name=name, scratch_shapes=scratch, input_output_aliases=aliases,
            compiler_params=pltpu.CompilerParams(vmem_limit_bytes=4 << 20),
            cost_estimate=pl.CostEstimate(flops=2 * dots * B ** 3, bytes_accessed=(4 << 20) * (dots > 0), transcendentals=0))

    ends = pl.BlockSpec((QMAX, B, B), lambda i: (0, 0, 0)), pl.BlockSpec((QMAX, B, B), lambda i: (SECS // QMAX - 1, 0, 0))
    packed = jax.ShapeDtypeStruct((STRIP + QMAX * B, B), BF)
    whole = pl.BlockSpec((STRIP + QMAX * B, B), lambda i: (0, 0))
    dims_there = pltpu.with_memory_space_constraint(sector_dims, pltpu.HBM)
    right_there = pltpu.with_memory_space_constraint(right_ops, pltpu.HBM)
    psi_there = pltpu.with_memory_space_constraint(psi, pltpu.HBM)
    up, down = pl.pallas_call(
        pack, grid=(1,), in_specs=[smem, *ends, pl.BlockSpec((OPS, 16, B), lambda i: (0, 0, 0))],
        out_shape=[packed, packed], out_specs=[whole, whole], name="pack",
        compiler_params=pltpu.CompilerParams(vmem_limit_bytes=4 << 20),
        cost_estimate=pl.CostEstimate(flops=0, bytes_accessed=1 << 20, transcendentals=0),
    )(dims_there, psi_there, psi_there, pltpu.with_memory_space_constraint(left_ops, pltpu.HBM))
    place, left_ops, up = lax.optimization_barrier((place, left_ops, up))
    sent = up
    up = move(sent, gather_first(1))
    down = move(down, gather_first(-1))
    two = move(left_ops, gather_first(2))
    live_psi, right, h, done = call(
        first_operators, "first_operators", [smem, hbm, hbm],
        [((SECS, B, B), BF), ((OPS, B, B), BF), ((OPS, HELD * B, B), BF), ((8, 128), F32)], EARLY * SECS,
        [pltpu.SemaphoreType.DMA((SECS,)), pltpu.SemaphoreType.DMA],
    )(dims_there, psi_there, right_there)
    strips, = call(unpack, "unpack", [vmem] * 5, [((4, OPS, 16, B), BF)], 0)(sent, up, down, two, done)
    up_late, down_late, _ = lax.optimization_barrier((up, down, strips))
    up_other, down_other = move(up_late, other_core), move(down_late, other_core)
    seconds = [move(strips, gather_second(d)) for d in (2, 1, 3)]
    t0, t2, t1, t3 = strips, *seconds

    h, = call(
        other_sectors, "other_sectors", [smem, smem] + [vmem] * 7, [((OPS, HELD * B, B), BF)], 0,
        [pltpu.VMEM((2 * QMAX * B, B), BF)], {8: 0},
    )(op_shift, place, up, down, up_other, down_other, live_psi, right, h)

    first_a = [((NZ, SPLIT, 32, B), F32), ((NZ, SPLIT, 32, B), BF), ((B, OPS * B), BF)]
    mine_a, away_a, left = call(first_targets, "first_targets", [smem, smem] + [vmem] * 5, first_a, OPS * SPLIT)(
        op_shift, place, t0, t1, t2, t3, h)
    rest = [((NZ, SECS - SPLIT, 32, B), F32), ((NZ, SECS - SPLIT, 32, B), BF)]
    mine_b, away_b = call(
        functools.partial(some_targets, SPLIT), "last_targets", [smem, vmem, vmem], rest, OPS * (SECS - SPLIT),
    )(op_shift, left, h)

    slot = (SECS, 32, B)
    own, near, far, back = call(
        add_cores, "add_cores", [vmem] * 4, [(slot, F32), (slot, F32), (slot, BF), (slot, BF)], 0,
    )(mine_a, mine_b, move(away_a, other_core), move(away_b, other_core))
    far = move(far, along_z(1))
    back = move(back, along_z(-1))
    near = move((near + far.astype(F32)).astype(BF), along_z(1))
    summed = own + back.astype(F32) + near.astype(F32)
    index = jnp.arange(B, dtype=jnp.int32)
    live = index[None, :] < sector_dims[:, None]
    mine_rows = p * 32 + jnp.arange(32, dtype=jnp.int32)
    live_rows = mine_rows[None, :] < sector_dims[:, None]
    return jnp.where(live_rows[:, :, None] & live[:, None, :], summed, 0.0).astype(BF)


def solution(mesh):
    placed = (P("sec", None, None), P("op", "sec", None), P("op", None, None), P("op"), P("sec"))
    return jax.shard_map(
        on_device, mesh=mesh, in_specs=placed, out_specs=P("sec", "op", None), check_vma=False
    )
```

```python
import functools

import jax
import jax.numpy as jnp
from jax import lax
from jax.experimental import pallas as pl
from jax.experimental.pallas import tpu as pltpu
from jax.sharding import PartitionSpec as P

NZ, NC, NY, NX = 4, 2, 4, 4
B = 256
OPS = 8
SECS = 16
QMAX = 2
HELD = SECS + 2 * QMAX
STRIP = OPS * 16
EARLY = 6
SPLIT = 12
BF = jnp.bfloat16
F32 = jnp.float32


def flat(z, c, y, x):
    return ((z * NC + c) * NY + y) * NX + x


def move(block, target):
    route = []
    for z in range(NZ):
        for c in range(NC):
            for y in range(NY):
                for x in range(NX):
                    to = target(z, c, y, x)
                    if to is not None:
                        route.append((flat(z, c, y, x), flat(*to)))
    return lax.ppermute(block, ("op", "sec"), route)


def gather_first(d):
    def target(z, c, y, x):
        if c == 0:
            q = (y * NX + x + d) % SECS
            return (z, c, q // NX, q % NX)
        return (z, c, (y + d) % NY, x)

    return target


def gather_second(d):
    return lambda z, c, y, x: (z, c, (y + d) % NY, x) if c == 0 else (z, c, y, (x + d) % NX)


def other_core(z, c, y, x):
    return (z, 1 - c, y, x)


def along_z(sign):
    return lambda z, c, y, x: ((z + (sign if c == 0 else -sign)) % NZ, c, y, x)


def masked(block, d):
    rows = lax.broadcasted_iota(jnp.int32, (B, B), 0)
    cols = lax.broadcasted_iota(jnp.int32, (B, B), 1)
    return jnp.where((rows < d) & (cols < d), block.astype(F32), 0.0).astype(BF)


def pack(dims_ref, first_psi, last_psi, left_ref, up_ref, down_ref):
    strip = left_ref[...].reshape(STRIP, B)
    up_ref[:STRIP, :] = strip
    down_ref[:STRIP, :] = strip
    for e in range(QMAX):
        to = slice(STRIP + e * B, STRIP + (e + 1) * B)
        up_ref[to, :] = masked(last_psi[e], dims_ref[SECS - QMAX + e])
        down_ref[to, :] = masked(first_psi[e], dims_ref[e])


def unpack(own, from_below, from_above, second_below, after, strips_ref):
    strips_ref[0] = own[:STRIP, :].reshape(OPS, 16, B)
    strips_ref[1] = from_below[:STRIP, :].reshape(OPS, 16, B)
    strips_ref[2] = from_above[:STRIP, :].reshape(OPS, 16, B)
    strips_ref[3] = second_below[...]


def by_twos(one, ops=(0, OPS)):
    def two_operators(i, _):
        one(2 * i)
        one(2 * i + 1)
        return 0

    lax.fori_loop(ops[0] // 2, ops[1] // 2, two_operators, 0)


def own_sectors(ops, masked_ref, right_ref, *refs):
    h_ref = refs[-1]

    def one_operator(o):
        right_t = right_ref[o].T
        for s in range(0, SECS, 4):
            h = jnp.dot(masked_ref[s:s + 4].reshape(4 * B, B), right_t, preferred_element_type=F32)
            h_ref[o, (s + QMAX) * B:(s + QMAX + 4) * B, :] = h.astype(BF)

    by_twos(one_operator, ops)


def first_operators(dims_ref, psi_ref, right_ref, masked_ref, h_ref, done_ref):
    def mask_one(s, _):
        masked_ref[s] = masked(psi_ref[s], dims_ref[s])
        return 0

    lax.fori_loop(0, SECS, mask_one, 0)
    own_sectors((0, EARLY), masked_ref, right_ref, h_ref)
    done_ref[...] = jnp.zeros_like(done_ref)


def other_sectors(shift_ref, place_ref, below_0, above_0, below_1, above_1, masked_ref, right_ref, _, h_ref, edge_ref):
    core = place_ref[1]
    q = place_ref[2] * NX + place_ref[3]
    for k, (sources, present) in enumerate((((below_0, below_1), q > 0), ((above_0, above_1), q < SECS - 1))):
        to = slice(k * QMAX * B, (k + 1) * QMAX * B)
        for c, source in enumerate(sources):

            @pl.when(present & (core == c))
            def _():
                edge_ref[to, :] = source[STRIP:, :]

        @pl.when(jnp.logical_not(present))
        def _():
            edge_ref[to, :] = jnp.zeros((QMAX * B, B), BF)

    def edge_side(o):
        above = (shift_ref[o] < 0).astype(jnp.int32)
        source = pl.multiple_of(above * (QMAX * B), QMAX * B)
        to = pl.multiple_of(above * ((QMAX + SECS) * B), QMAX * B)
        h = jnp.dot(edge_ref[pl.ds(source, QMAX * B), :], right_ref[o].T, preferred_element_type=F32)
        h_ref[o, pl.ds(to, QMAX * B), :] = h.astype(BF)

    own_sectors((EARLY, OPS), masked_ref, right_ref, h_ref)
    for o in range(OPS):
        edge_side(o)


def order_left(place_ref, t0, t1, t2, t3, left_ref):
    z, core, y, x = place_ref[0], place_ref[1], place_ref[2], place_ref[3]
    for e, block in enumerate((t0, t1, t2, t3)):
        for d in range(4):
            step = (0, -1, 1, -2)[d]
            along_ring = (y * NX + x + step - e * NX + 2 * SECS) % SECS
            along_y = (y + step + NY) % NY * NX + (x - e + NX) % NX
            q = jnp.where(core == 0, along_ring, along_y)
            to_z, to_core = q // 4, (q // 2) % 2
            ahead = jnp.where(to_core == 0, to_z - z + NZ, z - to_z + NZ) % NZ
            start = jnp.where(to_core == core, 0, B // 2) + ahead * 32 + (q % 2) * 16
            start = pl.multiple_of(start, 16)
            for o in range(OPS):
                left_ref[pl.ds(start, 16), o * B:(o + 1) * B] = block[d, o]


def some_targets(first, shift_ref, left_ref, h_ref, mine_ref, other_ref):
    count = mine_ref.shape[1]
    at_once = min(count, 6)

    def several_targets(i, _):
        for u in range(at_once):
            t = i * at_once + u
            sources = [
                h_ref[o, pl.ds(pl.multiple_of((first + t + QMAX - shift_ref[o]) * B, B), B), :] for o in range(OPS)
            ]
            total = jnp.dot(left_ref[...], jnp.concatenate(sources, axis=0), preferred_element_type=F32)
            for k in range(NZ):
                mine_ref[k, t] = total[k * 32:(k + 1) * 32]
                other_ref[k, t] = total[B // 2 + k * 32:B // 2 + (k + 1) * 32].astype(BF)
        return 0

    lax.fori_loop(0, count // at_once, several_targets, 0)


def first_targets(shift_ref, place_ref, t0, t1, t2, t3, h_ref, mine_ref, other_ref, left_ref):
    order_left(place_ref, t0, t1, t2, t3, left_ref)
    some_targets(0, shift_ref, left_ref, h_ref, mine_ref, other_ref)


def add_cores(mine_a, mine_b, got_a, got_b, own_ref, near_ref, far_ref, back_ref):
    for mine, got, to in ((mine_a, got_a, slice(0, SPLIT)), (mine_b, got_b, slice(SPLIT, SECS))):
        own_ref[to] = mine[0] + got[0].astype(F32)
        near_ref[to] = mine[1] + got[1].astype(F32)
        far_ref[to] = (mine[2] + got[2].astype(F32)).astype(BF)
        back_ref[to] = (mine[3] + got[3].astype(F32)).astype(BF)


def on_device(psi, left_ops, right_ops, op_shift, sector_dims):
    p, q = lax.axis_index("op"), lax.axis_index("sec")
    core = p % NC
    place = jnp.stack([p // NC, core, q // NX, q % NX]).astype(jnp.int32)

    smem = pl.BlockSpec(memory_space=pltpu.SMEM)
    vmem = pl.BlockSpec(memory_space=pltpu.VMEM)


    def call(kernel, name, in_specs, out_shape, dots, scratch=(), aliases={}):
        return pl.pallas_call(
            kernel, in_specs=in_specs, out_shape=[jax.ShapeDtypeStruct(*o) for o in out_shape],
            out_specs=[vmem] * len(out_shape), name=name, scratch_shapes=scratch, input_output_aliases=aliases,
            compiler_params=pltpu.CompilerParams(vmem_limit_bytes=4 << 20),
            cost_estimate=pl.CostEstimate(flops=2 * dots * B ** 3, bytes_accessed=(4 << 20) * (dots > 0), transcendentals=0))

    ends = pl.BlockSpec((QMAX, B, B), lambda i: (0, 0, 0)), pl.BlockSpec((QMAX, B, B), lambda i: (SECS // QMAX - 1, 0, 0))
    packed = jax.ShapeDtypeStruct((STRIP + QMAX * B, B), BF)
    whole = pl.BlockSpec((STRIP + QMAX * B, B), lambda i: (0, 0))
    dims_there = pltpu.with_memory_space_constraint(sector_dims, pltpu.HBM)
    right_there = pltpu.with_memory_space_constraint(right_ops, pltpu.HBM)
    psi_there = pltpu.with_memory_space_constraint(psi, pltpu.HBM)
    up, down = pl.pallas_call(
        pack, grid=(1,), in_specs=[smem, *ends, pl.BlockSpec((OPS, 16, B), lambda i: (0, 0, 0))],
        out_shape=[packed, packed], out_specs=[whole, whole], name="pack",
        compiler_params=pltpu.CompilerParams(vmem_limit_bytes=4 << 20),
        cost_estimate=pl.CostEstimate(flops=0, bytes_accessed=1 << 20, transcendentals=0),
    )(dims_there, psi_there, psi_there, pltpu.with_memory_space_constraint(left_ops, pltpu.HBM))
    place, left_ops, up = lax.optimization_barrier((place, left_ops, up))
    sent = up
    up = move(sent, gather_first(1))
    down = move(down, gather_first(-1))
    two = move(left_ops, gather_first(2))
    live_psi, h, done = call(
        first_operators, "first_operators", [smem, vmem, vmem],
        [((SECS, B, B), BF), ((OPS, HELD * B, B), BF), ((8, 128), F32)], EARLY * SECS,
    )(dims_there, psi, right_ops)
    strips, = call(unpack, "unpack", [vmem] * 5, [((4, OPS, 16, B), BF)], 0)(sent, up, down, two, done)
    up_late, down_late, _ = lax.optimization_barrier((up, down, strips))
    up_other, down_other = move(up_late, other_core), move(down_late, other_core)
    seconds = [move(strips, gather_second(d)) for d in (2, 1, 3)]
    t0, t2, t1, t3 = strips, *seconds

    h, = call(
        other_sectors, "other_sectors", [smem, smem] + [vmem] * 7, [((OPS, HELD * B, B), BF)], 0,
        [pltpu.VMEM((2 * QMAX * B, B), BF)], {8: 0},
    )(op_shift, place, up, down, up_other, down_other, live_psi, right_ops, h)

    first_a = [((NZ, SPLIT, 32, B), F32), ((NZ, SPLIT, 32, B), BF), ((B, OPS * B), BF)]
    mine_a, away_a, left = call(first_targets, "first_targets", [smem, smem] + [vmem] * 5, first_a, OPS * SPLIT)(
        op_shift, place, t0, t1, t2, t3, h)
    rest = [((NZ, SECS - SPLIT, 32, B), F32), ((NZ, SECS - SPLIT, 32, B), BF)]
    mine_b, away_b = call(
        functools.partial(some_targets, SPLIT), "last_targets", [smem, vmem, vmem], rest, OPS * (SECS - SPLIT),
    )(op_shift, left, h)

    slot = (SECS, 32, B)
    own, near, far, back = call(
        add_cores, "add_cores", [vmem] * 4, [(slot, F32), (slot, F32), (slot, BF), (slot, BF)], 0,
    )(mine_a, mine_b, move(away_a, other_core), move(away_b, other_core))
    far = move(far, along_z(1))
    back = move(back, along_z(-1))
    near = move((near + far.astype(F32)).astype(BF), along_z(1))
    summed = own + back.astype(F32) + near.astype(F32)
    index = jnp.arange(B, dtype=jnp.int32)
    live = index[None, :] < sector_dims[:, None]
    mine_rows = p * 32 + jnp.arange(32, dtype=jnp.int32)
    live_rows = mine_rows[None, :] < sector_dims[:, None]
    return jnp.where(live_rows[:, :, None] & live[:, None, :], summed, 0.0).astype(BF)


def solution(mesh):
    placed = (P("sec", None, None), P("op", "sec", None), P("op", None, None), P("op"), P("sec"))
    return jax.shard_map(
        on_device, mesh=mesh, in_specs=placed, out_specs=P("sec", "op", None), check_vma=False
    )
```

```python
import functools

import jax
import jax.numpy as jnp
from jax import lax
from jax.experimental import pallas as pl
from jax.experimental.pallas import tpu as pltpu
from jax.sharding import PartitionSpec as P

NZ, NC, NY, NX = 4, 2, 4, 4
B = 256
OPS = 8
SECS = 16
QMAX = 2
HELD = SECS + 2 * QMAX
STRIP = OPS * 16
EARLY = 4
SPLIT = 8
BF = jnp.bfloat16
F32 = jnp.float32


def flat(z, c, y, x):
    return ((z * NC + c) * NY + y) * NX + x


def move(block, target):
    route = []
    for z in range(NZ):
        for c in range(NC):
            for y in range(NY):
                for x in range(NX):
                    to = target(z, c, y, x)
                    if to is not None:
                        route.append((flat(z, c, y, x), flat(*to)))
    return lax.ppermute(block, ("op", "sec"), route)


def gather_first(d):
    def target(z, c, y, x):
        if c == 0:
            q = (y * NX + x + d) % SECS
            return (z, c, q // NX, q % NX)
        return (z, c, (y + d) % NY, x)

    return target


def gather_second(d):
    return lambda z, c, y, x: (z, c, (y + d) % NY, x) if c == 0 else (z, c, y, (x + d) % NX)


def other_core(z, c, y, x):
    return (z, 1 - c, y, x)


def along_z(sign):
    return lambda z, c, y, x: ((z + (sign if c == 0 else -sign)) % NZ, c, y, x)


def masked(block, d):
    rows = lax.broadcasted_iota(jnp.int32, (B, B), 0)
    cols = lax.broadcasted_iota(jnp.int32, (B, B), 1)
    return jnp.where((rows < d) & (cols < d), block.astype(F32), 0.0).astype(BF)


def pack(dims_ref, first_psi, last_psi, left_ref, up_ref, down_ref):
    strip = left_ref[...].reshape(STRIP, B)
    up_ref[:STRIP, :] = strip
    down_ref[:STRIP, :] = strip
    for e in range(QMAX):
        to = slice(STRIP + e * B, STRIP + (e + 1) * B)
        up_ref[to, :] = masked(last_psi[e], dims_ref[SECS - QMAX + e])
        down_ref[to, :] = masked(first_psi[e], dims_ref[e])


def unpack(own, from_below, from_above, second_below, after, strips_ref):
    strips_ref[0] = own[:STRIP, :].reshape(OPS, 16, B)
    strips_ref[1] = from_below[:STRIP, :].reshape(OPS, 16, B)
    strips_ref[2] = from_above[:STRIP, :].reshape(OPS, 16, B)
    strips_ref[3] = second_below[...]


def by_twos(one, ops=(0, OPS)):
    def two_operators(i, _):
        one(2 * i)
        one(2 * i + 1)
        return 0

    lax.fori_loop(ops[0] // 2, ops[1] // 2, two_operators, 0)


def own_sectors(ops, masked_ref, right_ref, *refs):
    h_ref = refs[-1]

    def one_operator(o):
        right_t = right_ref[o].T
        for s in range(0, SECS, 4):
            h = jnp.dot(masked_ref[s:s + 4].reshape(4 * B, B), right_t, preferred_element_type=F32)
            h_ref[o, (s + QMAX) * B:(s + QMAX + 4) * B, :] = h.astype(BF)

    by_twos(one_operator, ops)


def first_operators(dims_ref, psi_hbm, right_hbm, masked_ref, right_ref, h_ref, done_ref, psi_sem, right_sem):
    right_in = pltpu.make_async_copy(right_hbm, right_ref, right_sem)

    def psi_in(s):
        return pltpu.make_async_copy(psi_hbm.at[s], masked_ref.at[s], psi_sem.at[s])

    for s in range(SECS):
        psi_in(s).start()
    right_in.start()

    def mask_one(s, _):
        psi_in(s).wait()
        masked_ref[s] = masked(masked_ref[s], dims_ref[s])
        return 0

    lax.fori_loop(0, SECS, mask_one, 0)
    right_in.wait()
    own_sectors((0, EARLY), masked_ref, right_ref, h_ref)
    done_ref[...] = jnp.zeros_like(done_ref)


def other_sectors(shift_ref, place_ref, below_0, above_0, below_1, above_1, masked_ref, right_ref, _, h_ref, edge_ref):
    core = place_ref[1]
    q = place_ref[2] * NX + place_ref[3]
    for k, (sources, present) in enumerate((((below_0, below_1), q > 0), ((above_0, above_1), q < SECS - 1))):
        to = slice(k * QMAX * B, (k + 1) * QMAX * B)
        for c, source in enumerate(sources):

            @pl.when(present & (core == c))
            def _():
                edge_ref[to, :] = source[STRIP:, :]

        @pl.when(jnp.logical_not(present))
        def _():
            edge_ref[to, :] = jnp.zeros((QMAX * B, B), BF)

    def edge_side(o):
        above = (shift_ref[o] < 0).astype(jnp.int32)
        source = pl.multiple_of(above * (QMAX * B), QMAX * B)
        to = pl.multiple_of(above * ((QMAX + SECS) * B), QMAX * B)
        h = jnp.dot(edge_ref[pl.ds(source, QMAX * B), :], right_ref[o].T, preferred_element_type=F32)
        h_ref[o, pl.ds(to, QMAX * B), :] = h.astype(BF)

    own_sectors((EARLY, OPS), masked_ref, right_ref, h_ref)
    for o in range(OPS):
        edge_side(o)


def order_left(place_ref, t0, t1, t2, t3, left_ref):
    z, core, y, x = place_ref[0], place_ref[1], place_ref[2], place_ref[3]
    for e, block in enumerate((t0, t1, t2, t3)):
        for d in range(4):
            step = (0, -1, 1, -2)[d]
            along_ring = (y * NX + x + step - e * NX + 2 * SECS) % SECS
            along_y = (y + step + NY) % NY * NX + (x - e + NX) % NX
            q = jnp.where(core == 0, along_ring, along_y)
            to_z, to_core = q // 4, (q // 2) % 2
            ahead = jnp.where(to_core == 0, to_z - z + NZ, z - to_z + NZ) % NZ
            start = jnp.where(to_core == core, 0, B // 2) + ahead * 32 + (q % 2) * 16
            start = pl.multiple_of(start, 16)
            for o in range(OPS):
                left_ref[pl.ds(start, 16), o * B:(o + 1) * B] = block[d, o]


def some_targets(first, shift_ref, left_ref, h_ref, mine_ref, other_ref):
    count = mine_ref.shape[1]
    at_once = min(count, 8)

    def several_targets(i, _):
        for u in range(at_once):
            t = i * at_once + u
            sources = [
                h_ref[o, pl.ds(pl.multiple_of((first + t + QMAX - shift_ref[o]) * B, B), B), :] for o in range(OPS)
            ]
            total = jnp.dot(left_ref[...], jnp.concatenate(sources, axis=0), preferred_element_type=F32)
            for k in range(NZ):
                mine_ref[k, t] = total[k * 32:(k + 1) * 32]
                other_ref[k, t] = total[B // 2 + k * 32:B // 2 + (k + 1) * 32].astype(BF)
        return 0

    lax.fori_loop(0, count // at_once, several_targets, 0)


def first_targets(shift_ref, place_ref, t0, t1, t2, t3, h_ref, mine_ref, other_ref, left_ref):
    order_left(place_ref, t0, t1, t2, t3, left_ref)
    some_targets(0, shift_ref, left_ref, h_ref, mine_ref, other_ref)


def add_cores(mine_a, mine_b, got_a, got_b, own_ref, near_ref, far_ref, back_ref):
    for mine, got, to in ((mine_a, got_a, slice(0, SPLIT)), (mine_b, got_b, slice(SPLIT, SECS))):
        own_ref[to] = mine[0] + got[0].astype(F32)
        near_ref[to] = mine[1] + got[1].astype(F32)
        far_ref[to] = (mine[2] + got[2].astype(F32)).astype(BF)
        back_ref[to] = (mine[3] + got[3].astype(F32)).astype(BF)


def on_device(psi, left_ops, right_ops, op_shift, sector_dims):
    p, q = lax.axis_index("op"), lax.axis_index("sec")
    core = p % NC
    place = jnp.stack([p // NC, core, q // NX, q % NX]).astype(jnp.int32)

    smem = pl.BlockSpec(memory_space=pltpu.SMEM)
    vmem = pl.BlockSpec(memory_space=pltpu.VMEM)
    hbm = pl.BlockSpec(memory_space=pltpu.HBM)

    def call(kernel, name, in_specs, out_shape, dots, scratch=(), aliases={}):
        return pl.pallas_call(
            kernel, in_specs=in_specs, out_shape=[jax.ShapeDtypeStruct(*o) for o in out_shape],
            out_specs=[vmem] * len(out_shape), name=name, scratch_shapes=scratch, input_output_aliases=aliases,
            compiler_params=pltpu.CompilerParams(vmem_limit_bytes=4 << 20),
            cost_estimate=pl.CostEstimate(flops=2 * dots * B ** 3, bytes_accessed=(4 << 20) * (dots > 0), transcendentals=0))

    ends = pl.BlockSpec((QMAX, B, B), lambda i: (0, 0, 0)), pl.BlockSpec((QMAX, B, B), lambda i: (SECS // QMAX - 1, 0, 0))
    packed = jax.ShapeDtypeStruct((STRIP + QMAX * B, B), BF)
    whole = pl.BlockSpec((STRIP + QMAX * B, B), lambda i: (0, 0))
    dims_there = pltpu.with_memory_space_constraint(sector_dims, pltpu.HBM)
    right_there = pltpu.with_memory_space_constraint(right_ops, pltpu.HBM)
    psi_there = pltpu.with_memory_space_constraint(psi, pltpu.HBM)
    up, down = pl.pallas_call(
        pack, grid=(1,), in_specs=[smem, *ends, pl.BlockSpec((OPS, 16, B), lambda i: (0, 0, 0))],
        out_shape=[packed, packed], out_specs=[whole, whole], name="pack",
        compiler_params=pltpu.CompilerParams(vmem_limit_bytes=4 << 20),
        cost_estimate=pl.CostEstimate(flops=0, bytes_accessed=1 << 20, transcendentals=0),
    )(dims_there, psi_there, psi_there, pltpu.with_memory_space_constraint(left_ops, pltpu.HBM))
    place, left_ops, up = lax.optimization_barrier((place, left_ops, up))
    sent = up
    up = move(sent, gather_first(1))
    down = move(down, gather_first(-1))
    two = move(left_ops, gather_first(2))
    live_psi, right, h, done = call(
        first_operators, "first_operators", [smem, hbm, hbm],
        [((SECS, B, B), BF), ((OPS, B, B), BF), ((OPS, HELD * B, B), BF), ((8, 128), F32)], EARLY * SECS,
        [pltpu.SemaphoreType.DMA((SECS,)), pltpu.SemaphoreType.DMA],
    )(dims_there, psi_there, right_there)
    strips, = call(unpack, "unpack", [vmem] * 5, [((4, OPS, 16, B), BF)], 0)(sent, up, down, two, done)
    up_late, down_late, _ = lax.optimization_barrier((up, down, strips))
    up_other, down_other = move(up_late, other_core), move(down_late, other_core)
    seconds = [move(strips, gather_second(d)) for d in (2, 1, 3)]
    t0, t2, t1, t3 = strips, *seconds

    h, = call(
        other_sectors, "other_sectors", [smem, smem] + [vmem] * 7, [((OPS, HELD * B, B), BF)], 0,
        [pltpu.VMEM((2 * QMAX * B, B), BF)], {8: 0},
    )(op_shift, place, up, down, up_other, down_other, live_psi, right, h)

    first_a = [((NZ, SPLIT, 32, B), F32), ((NZ, SPLIT, 32, B), BF), ((B, OPS * B), BF)]
    mine_a, away_a, left = call(first_targets, "first_targets", [smem, smem] + [vmem] * 5, first_a, OPS * SPLIT)(
        op_shift, place, t0, t1, t2, t3, h)
    rest = [((NZ, SECS - SPLIT, 32, B), F32), ((NZ, SECS - SPLIT, 32, B), BF)]
    mine_b, away_b = call(
        functools.partial(some_targets, SPLIT), "last_targets", [smem, vmem, vmem], rest, OPS * (SECS - SPLIT),
    )(op_shift, left, h)

    slot = (SECS, 32, B)
    own, near, far, back = call(
        add_cores, "add_cores", [vmem] * 4, [(slot, F32), (slot, F32), (slot, BF), (slot, BF)], 0,
    )(mine_a, mine_b, move(away_a, other_core), move(away_b, other_core))
    far = move(far, along_z(1))
    back = move(back, along_z(-1))
    near = move((near + far.astype(F32)).astype(BF), along_z(1))
    summed = own + back.astype(F32) + near.astype(F32)
    index = jnp.arange(B, dtype=jnp.int32)
    live = index[None, :] < sector_dims[:, None]
    mine_rows = p * 32 + jnp.arange(32, dtype=jnp.int32)
    live_rows = mine_rows[None, :] < sector_dims[:, None]
    return jnp.where(live_rows[:, :, None] & live[:, None, :], summed, 0.0).astype(BF)


def solution(mesh):
    placed = (P("sec", None, None), P("op", "sec", None), P("op", None, None), P("op"), P("sec"))
    return jax.shard_map(
        on_device, mesh=mesh, in_specs=placed, out_specs=P("sec", "op", None), check_vma=False
    )
```

```python
import functools

import jax
import jax.numpy as jnp
from jax import lax
from jax.experimental import pallas as pl
from jax.experimental.pallas import tpu as pltpu
from jax.sharding import PartitionSpec as P

NZ, NC, NY, NX = 4, 2, 4, 4
B = 256
OPS = 8
SECS = 16
QMAX = 2
HELD = SECS + 2 * QMAX
STRIP = OPS * 16
EARLY = 4
SPLIT = 12
BF = jnp.bfloat16
F32 = jnp.float32


def flat(z, c, y, x):
    return ((z * NC + c) * NY + y) * NX + x


def move(block, target):
    route = []
    for z in range(NZ):
        for c in range(NC):
            for y in range(NY):
                for x in range(NX):
                    to = target(z, c, y, x)
                    if to is not None:
                        route.append((flat(z, c, y, x), flat(*to)))
    return lax.ppermute(block, ("op", "sec"), route)


def gather_first(d):
    def target(z, c, y, x):
        if c == 0:
            q = (y * NX + x + d) % SECS
            return (z, c, q // NX, q % NX)
        return (z, c, (y + d) % NY, x)

    return target


def gather_second(d):
    return lambda z, c, y, x: (z, c, (y + d) % NY, x) if c == 0 else (z, c, y, (x + d) % NX)


def other_core(z, c, y, x):
    return (z, 1 - c, y, x)


def along_z(sign):
    return lambda z, c, y, x: ((z + (sign if c == 0 else -sign)) % NZ, c, y, x)


def masked(block, d):
    rows = lax.broadcasted_iota(jnp.int32, (B, B), 0)
    cols = lax.broadcasted_iota(jnp.int32, (B, B), 1)
    return jnp.where((rows < d) & (cols < d), block.astype(F32), 0.0).astype(BF)


def pack(dims_ref, first_psi, last_psi, left_ref, up_ref, down_ref):
    strip = left_ref[...].reshape(STRIP, B)
    up_ref[:STRIP, :] = strip
    down_ref[:STRIP, :] = strip
    for e in range(QMAX):
        to = slice(STRIP + e * B, STRIP + (e + 1) * B)
        up_ref[to, :] = masked(last_psi[e], dims_ref[SECS - QMAX + e])
        down_ref[to, :] = masked(first_psi[e], dims_ref[e])


def unpack(own, from_below, from_above, second_below, after, strips_ref):
    strips_ref[0] = own[:STRIP, :].reshape(OPS, 16, B)
    strips_ref[1] = from_below[:STRIP, :].reshape(OPS, 16, B)
    strips_ref[2] = from_above[:STRIP, :].reshape(OPS, 16, B)
    strips_ref[3] = second_below[...]


def by_twos(one, ops=(0, OPS)):
    def two_operators(i, _):
        one(2 * i)
        one(2 * i + 1)
        return 0

    lax.fori_loop(ops[0] // 2, ops[1] // 2, two_operators, 0)


def own_sectors(ops, masked_ref, right_ref, *refs):
    h_ref = refs[-1]

    def one_operator(o):
        right_t = right_ref[o].T
        for s in range(0, SECS, 4):
            h = jnp.dot(masked_ref[s:s + 4].reshape(4 * B, B), right_t, preferred_element_type=F32)
            h_ref[o, (s + QMAX) * B:(s + QMAX + 4) * B, :] = h.astype(BF)

    by_twos(one_operator, ops)


def first_operators(dims_ref, psi_hbm, right_hbm, masked_ref, right_ref, h_ref, done_ref, psi_sem, right_sem):
    right_in = pltpu.make_async_copy(right_hbm, right_ref, right_sem)

    def psi_in(s):
        return pltpu.make_async_copy(psi_hbm.at[s], masked_ref.at[s], psi_sem.at[s])

    for s in range(SECS):
        psi_in(s).start()
    right_in.start()

    def mask_one(s, _):
        psi_in(s).wait()
        masked_ref[s] = masked(masked_ref[s], dims_ref[s])
        return 0

    lax.fori_loop(0, SECS, mask_one, 0)
    right_in.wait()
    own_sectors((0, EARLY), masked_ref, right_ref, h_ref)
    done_ref[...] = jnp.zeros_like(done_ref)


def other_sectors(shift_ref, place_ref, below_0, above_0, below_1, above_1, masked_ref, right_ref, _, h_ref, edge_ref):
    core = place_ref[1]
    q = place_ref[2] * NX + place_ref[3]
    for k, (sources, present) in enumerate((((below_0, below_1), q > 0), ((above_0, above_1), q < SECS - 1))):
        to = slice(k * QMAX * B, (k + 1) * QMAX * B)
        for c, source in enumerate(sources):

            @pl.when(present & (core == c))
            def _():
                edge_ref[to, :] = source[STRIP:, :]

        @pl.when(jnp.logical_not(present))
        def _():
            edge_ref[to, :] = jnp.zeros((QMAX * B, B), BF)

    def edge_side(o):
        above = (shift_ref[o] < 0).astype(jnp.int32)
        source = pl.multiple_of(above * (QMAX * B), QMAX * B)
        to = pl.multiple_of(above * ((QMAX + SECS) * B), QMAX * B)
        h = jnp.dot(edge_ref[pl.ds(source, QMAX * B), :], right_ref[o].T, preferred_element_type=F32)
        h_ref[o, pl.ds(to, QMAX * B), :] = h.astype(BF)

    own_sectors((EARLY, OPS), masked_ref, right_ref, h_ref)
    for o in range(OPS):
        edge_side(o)


def order_left(place_ref, t0, t1, t2, t3, left_ref):
    z, core, y, x = place_ref[0], place_ref[1], place_ref[2], place_ref[3]
    for e, block in enumerate((t0, t1, t2, t3)):
        for d in range(4):
            step = (0, -1, 1, -2)[d]
            along_ring = (y * NX + x + step - e * NX + 2 * SECS) % SECS
            along_y = (y + step + NY) % NY * NX + (x - e + NX) % NX
            q = jnp.where(core == 0, along_ring, along_y)
            to_z, to_core = q // 4, (q // 2) % 2
            ahead = jnp.where(to_core == 0, to_z - z + NZ, z - to_z + NZ) % NZ
            start = jnp.where(to_core == core, 0, B // 2) + ahead * 32 + (q % 2) * 16
            start = pl.multiple_of(start, 16)
            for o in range(OPS):
                left_ref[pl.ds(start, 16), o * B:(o + 1) * B] = block[d, o]


def some_targets(first, shift_ref, left_ref, h_ref, mine_ref, other_ref):
    count = mine_ref.shape[1]
    at_once = min(count, 6)

    def several_targets(i, _):
        for u in range(at_once):
            t = i * at_once + u
            sources = [
                h_ref[o, pl.ds(pl.multiple_of((first + t + QMAX - shift_ref[o]) * B, B), B), :] for o in range(OPS)
            ]
            total = jnp.dot(left_ref[...], jnp.concatenate(sources, axis=0), preferred_element_type=F32)
            for k in range(NZ):
                mine_ref[k, t] = total[k * 32:(k + 1) * 32]
                other_ref[k, t] = total[B // 2 + k * 32:B // 2 + (k + 1) * 32].astype(BF)
        return 0

    lax.fori_loop(0, count // at_once, several_targets, 0)


def first_targets(shift_ref, place_ref, t0, t1, t2, t3, h_ref, mine_ref, other_ref, left_ref):
    order_left(place_ref, t0, t1, t2, t3, left_ref)
    some_targets(0, shift_ref, left_ref, h_ref, mine_ref, other_ref)


def add_cores(mine_a, mine_b, got_a, got_b, own_ref, near_ref, far_ref, back_ref):
    for mine, got, to in ((mine_a, got_a, slice(0, SPLIT)), (mine_b, got_b, slice(SPLIT, SECS))):
        own_ref[to] = mine[0] + got[0].astype(F32)
        near_ref[to] = mine[1] + got[1].astype(F32)
        far_ref[to] = (mine[2] + got[2].astype(F32)).astype(BF)
        back_ref[to] = (mine[3] + got[3].astype(F32)).astype(BF)


def on_device(psi, left_ops, right_ops, op_shift, sector_dims):
    p, q = lax.axis_index("op"), lax.axis_index("sec")
    core = p % NC
    place = jnp.stack([p // NC, core, q // NX, q % NX]).astype(jnp.int32)

    smem = pl.BlockSpec(memory_space=pltpu.SMEM)
    vmem = pl.BlockSpec(memory_space=pltpu.VMEM)
    hbm = pl.BlockSpec(memory_space=pltpu.HBM)

    def call(kernel, name, in_specs, out_shape, dots, scratch=(), aliases={}):
        return pl.pallas_call(
            kernel, in_specs=in_specs, out_shape=[jax.ShapeDtypeStruct(*o) for o in out_shape],
            out_specs=[vmem] * len(out_shape), name=name, scratch_shapes=scratch, input_output_aliases=aliases,
            compiler_params=pltpu.CompilerParams(vmem_limit_bytes=4 << 20),
            cost_estimate=pl.CostEstimate(flops=2 * dots * B ** 3, bytes_accessed=(4 << 20) * (dots > 0), transcendentals=0))

    ends = pl.BlockSpec((QMAX, B, B), lambda i: (0, 0, 0)), pl.BlockSpec((QMAX, B, B), lambda i: (SECS // QMAX - 1, 0, 0))
    packed = jax.ShapeDtypeStruct((STRIP + QMAX * B, B), BF)
    whole = pl.BlockSpec((STRIP + QMAX * B, B), lambda i: (0, 0))
    dims_there = pltpu.with_memory_space_constraint(sector_dims, pltpu.HBM)
    right_there = pltpu.with_memory_space_constraint(right_ops, pltpu.HBM)
    psi_there = pltpu.with_memory_space_constraint(psi, pltpu.HBM)
    up, down = pl.pallas_call(
        pack, grid=(1,), in_specs=[smem, *ends, pl.BlockSpec((OPS, 16, B), lambda i: (0, 0, 0))],
        out_shape=[packed, packed], out_specs=[whole, whole], name="pack",
        compiler_params=pltpu.CompilerParams(vmem_limit_bytes=4 << 20),
        cost_estimate=pl.CostEstimate(flops=0, bytes_accessed=1 << 20, transcendentals=0),
    )(dims_there, psi_there, psi_there, pltpu.with_memory_space_constraint(left_ops, pltpu.HBM))
    place, left_ops, up = lax.optimization_barrier((place, left_ops, up))
    sent = up
    up = move(sent, gather_first(1))
    down = move(down, gather_first(-1))
    two = move(left_ops, gather_first(2))
    live_psi, right, h, done = call(
        first_operators, "first_operators", [smem, hbm, hbm],
        [((SECS, B, B), BF), ((OPS, B, B), BF), ((OPS, HELD * B, B), BF), ((8, 128), F32)], EARLY * SECS,
        [pltpu.SemaphoreType.DMA((SECS,)), pltpu.SemaphoreType.DMA],
    )(dims_there, psi_there, right_there)
    strips, = call(unpack, "unpack", [vmem] * 5, [((4, OPS, 16, B), BF)], 0)(sent, up, down, two, done)
    up_late, down_late, _ = lax.optimization_barrier((up, down, strips))
    up_other, down_other = move(up_late, other_core), move(down_late, other_core)
    seconds = [move(strips, gather_second(d)) for d in (2, 1, 3)]
    t0, t2, t1, t3 = strips, *seconds

    h, = call(
        other_sectors, "other_sectors", [smem, smem] + [vmem] * 7, [((OPS, HELD * B, B), BF)], 0,
        [pltpu.VMEM((2 * QMAX * B, B), BF)], {8: 0},
    )(op_shift, place, up, down, up_other, down_other, live_psi, right, h)

    first_a = [((NZ, SPLIT, 32, B), F32), ((NZ, SPLIT, 32, B), BF), ((B, OPS * B), BF)]
    mine_a, away_a, left = call(first_targets, "first_targets", [smem, smem] + [vmem] * 5, first_a, OPS * SPLIT)(
        op_shift, place, t0, t1, t2, t3, h)
    rest = [((NZ, SECS - SPLIT, 32, B), F32), ((NZ, SECS - SPLIT, 32, B), BF)]
    mine_b, away_b = call(
        functools.partial(some_targets, SPLIT), "last_targets", [smem, vmem, vmem], rest, OPS * (SECS - SPLIT),
    )(op_shift, left, h)

    slot = (SECS, 32, B)
    own, near, far, back = call(
        add_cores, "add_cores", [vmem] * 4, [(slot, F32), (slot, F32), (slot, BF), (slot, BF)], 0,
    )(mine_a, mine_b, move(away_a, other_core), move(away_b, other_core))
    far = move(far, along_z(1))
    back = move(back, along_z(-1))
    index = jnp.arange(B, dtype=jnp.int32)
    live_columns = (index[None, :] < sector_dims[:, None])[:, None, :]

    def live_at(chip):
        rows = (chip * NC + core) * 32 + jnp.arange(32, dtype=jnp.int32)
        return (rows[None, :] < sector_dims[:, None])[:, :, None] & live_columns

    next_chip = (place[0] + jnp.where(core == 0, 1, NZ - 1)) % NZ
    near = move(jnp.where(live_at(next_chip), near + far.astype(F32), 0.0).astype(BF), along_z(1))
    here = jnp.where(live_at(place[0]), own + back.astype(F32), 0.0)
    here = lax.optimization_barrier(here)
    return (here + near.astype(F32)).astype(BF)


def solution(mesh):
    placed = (P("sec", None, None), P("op", "sec", None), P("op", None, None), P("op"), P("sec"))
    return jax.shard_map(
        on_device, mesh=mesh, in_specs=placed, out_specs=P("sec", "op", None), check_vma=False
    )
```
